128 devices in a mesh: cp: 64 (over y, x, z), grp: 2 (over core).
Axes of the slice: x: 4, y: 4, z: 4, core: 2. Of those that a mesh axis runs over, the one named last changes fastest.
Arguments:
- queries: bfloat16 [16384, 640], P(('cp', 'grp')), may hold values from -24 to 24
- attn_keys: bfloat16 [16384, 128], P(('cp', 'grp')), may hold values from -24 to 24
- attn_values: bfloat16 [16384, 128], P(('cp', 'grp')), may hold values from -6 to 6
- out_grad: bfloat16 [16384, 640], P(('cp', 'grp')), may hold values from -6 to 6
- mask_ranges: int32 [13, 5], replicated, may hold values from 0 to 16384, as said below
- span_ids: int32 [256], replicated, may hold values from 0 to 255, as said below
Outputs:
- attn_out: bfloat16 [16384, 640], P(('cp', 'grp'))
- query_grad: bfloat16 [16384, 640], P(('cp', 'grp'))
- key_grad: bfloat16 [16384, 128], P(('cp', 'grp'))
- value_grad: bfloat16 [16384, 128], P(('cp', 'grp'))
The draws below stay inside these ranges and needn't reach their ends.
Inputs may be any that keep to these rules, and one draw needn't show every extreme that they name: `mask_ranges`: rows 0 to 3 are documents (b, e, b, e, 0) that tile the sequence in order, the first one the shared prefix; row 4 is (p, 16384, 0, p, 1) with p the prefix's end; the last 8 rows are images (s, s + 256, s, s + 256, 1). `span_ids`: each span appears once; the two span slots of one device hold spans c and 255 - c, in either order.
All inputs are finite; a program needn't handle non-finite values.
Results may differ from the reference program's by a relative error of at most 0.014.
Values may be sent and summed in bfloat16 or wider, within the bound.
No kernel may reach another device: no remote copies, remote signals or barrier semaphores. Data moves between devices by JAX's collectives and lax.ppermute only.
A program may use at most 128 MiB of HBM per device.

```python
import math
import jax
import jax.numpy as jnp
from jax import lax

GROUP_HEADS = 5
HEAD_DIM = 128
DOCS = 4
IMAGES = 8
SPAN = 64
SEQ = 16384
NCHUNK = 256
IMG_LEN = 256


def draw_queries(key, part):
    key = jax.random.fold_in(key, 1)
    result = jnp.clip(jax.random.normal(key, (SEQ, GROUP_HEADS * HEAD_DIM), jnp.float32), -6.0, 6.0)
    return result.astype(jnp.bfloat16)


def draw_attn_keys(key, part):
    key = jax.random.fold_in(key, 2)
    result = jnp.clip(jax.random.normal(key, (SEQ, HEAD_DIM), jnp.float32), -6.0, 6.0)
    return result.astype(jnp.bfloat16)


def draw_mask_ranges(key, part):
    key = jax.random.fold_in(key, 3)
    prefix_key, cut_key, image_key = jax.random.split(key, 3)
    lowest = SEQ // 8 + 1
    prefix_end = jax.random.randint(prefix_key, (1,), SEQ // 16, SEQ // 8 + 1).astype(jnp.int32)
    inner_cuts = jnp.sort(jax.random.permutation(cut_key, SEQ - lowest)[:DOCS - 2] + lowest).astype(jnp.int32)
    bounds = jnp.concatenate([jnp.zeros((1,), jnp.int32), prefix_end, inner_cuts, jnp.full((1,), SEQ, jnp.int32)])
    starts = bounds[:-1]
    doc_ends = bounds[1:]
    documents = jnp.stack([starts, doc_ends, starts, doc_ends, jnp.zeros_like(starts)], axis=1)
    shared = jnp.concatenate([prefix_end, jnp.array([SEQ, 0], jnp.int32), prefix_end, jnp.ones((1,), jnp.int32)])[None, :]
    image_starts = jax.random.randint(image_key, (IMAGES,), 0, SEQ - IMG_LEN + 1).astype(jnp.int32)
    images = jnp.stack([image_starts, image_starts + IMG_LEN, image_starts, image_starts + IMG_LEN, jnp.ones_like(image_starts)], axis=1)
    return jnp.concatenate([documents, shared, images], axis=0).astype(jnp.int32)


def draw_span_ids(key, part):
    key = jax.random.fold_in(key, 4)
    pair_key, flip_key = jax.random.split(key)
    half_count = NCHUNK // 2
    pairs = jax.random.permutation(pair_key, half_count).astype(jnp.int32)
    flips = jax.random.randint(flip_key, (half_count,), 0, 2).astype(jnp.int32)
    first = jnp.where(flips == 1, NCHUNK - 1 - pairs, pairs).astype(jnp.int32)
    second = (NCHUNK - 1 - first).astype(jnp.int32)
    return jnp.stack([first, second], axis=1).reshape(NCHUNK).astype(jnp.int32)


def steps_of(key, extent, shards, low, top_value):
    loudness, own = 1.0, jax.random.fold_in(key, 6)
    for axis_at, shards_of in shards:
        draws = jnp.exp(jax.random.uniform(jax.random.fold_in(own, axis_at), (shards_of,), jnp.float32, low / len(shards), top_value / len(shards)))
        loudness = loudness * jnp.repeat(draws, extent[axis_at] // shards_of).reshape([-1 if axis == axis_at else 1 for axis in range(len(extent))])
    return loudness


def normal_values(stream_key, dims, scale, limit, pieces=(), kind=jnp.bfloat16):
    factor_of = steps_of(stream_key, dims, pieces, -0.22, 0.18) if pieces else 1.0
    drawn = jax.random.normal(stream_key, dims, jnp.float32) * scale * factor_of
    return jnp.minimum(jnp.maximum(drawn, -limit), limit).astype(kind)


def setup_inputs(seed: int = 0) -> dict:
    streams_of = jax.random.split(jax.random.key(seed), 7)
    return {
        "queries": draw_queries(jax.random.fold_in(streams_of[6], 71), 0),
        "attn_keys": draw_attn_keys(jax.random.fold_in(streams_of[6], 71), 0),
        "attn_values": normal_values(streams_of[2], (SEQ, HEAD_DIM), 1.0, 6.0, ((0, 128),)),
        "out_grad": normal_values(streams_of[3], (SEQ, GROUP_HEADS * HEAD_DIM), 1.0, 6.0, ((0, 128),)),
        "mask_ranges": draw_mask_ranges(jax.random.fold_in(streams_of[6], 71), 0),
        "span_ids": draw_span_ids(jax.random.fold_in(streams_of[6], 71), 0),
    }


def key_positions(span_ids, first_row, row_count, span_len):
    row_index = first_row + jnp.arange(row_count, dtype=jnp.int32)
    return span_ids[row_index // span_len] * span_len + row_index % span_len

def visible_pairs(query_at, key_at, mask_ranges):
    bounds = [mask_ranges[:, column][:, None, None] for column in range(5)]
    query_wide = query_at[None, :, None]
    key_wide = key_at[None, None, :]
    covered = (query_wide >= bounds[0]) & (query_wide < bounds[1]) & (key_wide >= bounds[2]) & (key_wide < bounds[3])
    covered = covered & ((bounds[4] == 1) | (key_wide <= query_wide))
    return jnp.any(covered, axis=0)

def reference(queries, attn_keys, attn_values, out_grad, mask_ranges, span_ids):
    total_rows = queries.shape[0]
    softmax_scale = 1.0 / math.sqrt(HEAD_DIM)
    key_at = key_positions(span_ids, 0, total_rows, SPAN)
    block_len = math.gcd(total_rows, 256)
    block_count = total_rows // block_len
    query_blocks = queries.reshape(block_count, block_len, GROUP_HEADS, HEAD_DIM)
    grad_blocks = out_grad.reshape(block_count, block_len, GROUP_HEADS, HEAD_DIM)
    position_blocks = key_at.reshape(block_count, block_len)
    key_wide = attn_keys.astype(jnp.float32)
    value_wide = attn_values.astype(jnp.float32)

    def one_block(carried, blocks):
        key_total, value_total = carried
        query_block, grad_block, query_at = blocks
        query_wide = query_block.astype(jnp.float32)
        grad_wide = grad_block.astype(jnp.float32)
        seen_mask = visible_pairs(query_at, key_at, mask_ranges)[:, None, :]
        scores = jnp.einsum('thd,kd->thk', query_wide, key_wide) * softmax_scale
        row_max = lax.optimization_barrier(jnp.max(jnp.where(seen_mask, scores, -jnp.inf), axis=-1))
        row_sum = lax.optimization_barrier(jnp.sum(jnp.where(seen_mask, jnp.exp(scores - row_max[..., None]), 0.0), axis=-1))
        log_total = row_max + jnp.log(row_sum)
        probs_full = jnp.exp(jnp.where(seen_mask, scores - log_total[..., None], -jnp.inf))
        weights = probs_full.astype(jnp.bfloat16)
        weights_wide = weights.astype(jnp.float32)
        attn_block = jnp.einsum('thk,kd->thd', weights_wide, value_wide).astype(jnp.bfloat16)
        grad_dot = lax.optimization_barrier(jnp.sum(grad_wide * attn_block.astype(jnp.float32), axis=-1))
        prob_grad = jnp.einsum('thd,kd->thk', grad_wide, value_wide)
        dscore = (probs_full * (prob_grad - grad_dot[..., None])).astype(jnp.bfloat16)
        dscore_wide = dscore.astype(jnp.float32)
        query_block_grad = (jnp.einsum('thk,kd->thd', dscore_wide, key_wide) * softmax_scale).astype(jnp.bfloat16)
        key_total = key_total + jnp.einsum('thk,thd->kd', dscore_wide, query_wide) * softmax_scale
        value_total = value_total + jnp.einsum('thk,thd->kd', weights_wide, grad_wide)
        return ((key_total, value_total), (attn_block, query_block_grad))
    zero_total = jnp.zeros((total_rows, HEAD_DIM), jnp.float32)
    (key_total, value_total), (attn_blocks, query_grads) = lax.scan(one_block, (zero_total, zero_total), (query_blocks, grad_blocks, position_blocks))
    attn_out = attn_blocks.reshape(total_rows, GROUP_HEADS * HEAD_DIM)
    query_grad = query_grads.reshape(total_rows, GROUP_HEADS * HEAD_DIM)
    return (attn_out, query_grad, key_total.astype(jnp.bfloat16), value_total.astype(jnp.bfloat16))
```

```python
import functools
import math

import jax
import jax.numpy as jnp
from jax import lax
from jax.experimental import pallas as pl
from jax.experimental.pallas import tpu as pltpu
from jax.sharding import PartitionSpec as P

SIDE = 4
SPAN = 64
HEADS = 5
DIM = 128
PAIR = 2 * SPAN
LANES = HEADS * PAIR
PAIRS = SIDE
TILE = 256
TILE_SPANS = TILE // SPAN
PLANE = SIDE * SIDE
KEYS = 2 * PLANE * PAIR
KEY_SPANS = KEYS // SPAN
TILES = KEYS // TILE
FAR = -1e30
SCALE = 1.0 / math.sqrt(DIM)
LOG2_SCALE = SCALE * math.log2(math.e)
SHIFTS = (0, 1, -1, 2)
NT = (((1,), (1,)), ((), ()))
NN = (((1,), (0,)), ((), ()))


def dot(a, b, dims=NN):
    return lax.dot_general(a, b, dims, preferred_element_type=jnp.float32)


def flip(a):
    return jnp.transpose(a.astype(jnp.float32))


def seen(key_ids, pair, tile, key_feature, query_feature, query_at):
    cover = dot(key_feature[pl.ds(tile * TILE, TILE), :], query_feature[pair])
    row = lax.broadcasted_iota(jnp.int32, (SPAN, PAIR), 0)
    at = query_at[pair][0:1, :]
    past = jnp.concatenate(
        [row <= at - key_ids[tile * TILE_SPANS + s] * SPAN for s in range(TILE_SPANS)], axis=0
    )
    return cover > jnp.where(past, 0.5, 63.5)


def forward_kernel(
    live, key_ids, key_rank, query_rank,
    q0, q1, q2, q3, g0, g1, g2, g3, kv0, kv1, key_feature, query_feature, query_at,
    total_out, stat_out, q_sorted, g_sorted, k_sorted, v_sorted,
    v_turned, stat,
):
    for r, (q, g) in enumerate(zip((q0, q1, q2, q3), (g0, g1, g2, g3))):
        for s in range(2):
            rank = query_rank[2 * r + s]
            pair, half = rank // 2, lax.rem(rank, 2)
            for h in range(HEADS):
                to = pl.ds(pl.multiple_of(h * PAIR + half * SPAN, SPAN), SPAN)
                q_sorted[pair, to, :] = q[s * SPAN:(s + 1) * SPAN, h * DIM:(h + 1) * DIM]
                g_sorted[pair, to, :] = g[s * SPAN:(s + 1) * SPAN, h * DIM:(h + 1) * DIM]

    def sort_keys(i, _):
        for c, kv in enumerate((kv0, kv1)):
            for s in range(2):
                rank = key_rank[c * KEY_SPANS // 2 + 2 * i + s]
                to = pl.ds(pl.multiple_of(rank * SPAN, SPAN), SPAN)
                rows = kv[i][s * SPAN:(s + 1) * SPAN, :]
                k_sorted[to, :] = rows[:, :DIM]
                v_sorted[to, :] = rows[:, DIM:]
        return 0

    lax.fori_loop(0, PLANE, sort_keys, 0)

    def turn(t, _):
        at = pl.ds(pl.multiple_of(t * TILE, TILE), TILE)
        v_turned[t] = flip(v_sorted[at, :]).astype(jnp.bfloat16)
        return 0

    lax.fori_loop(0, TILES, turn, 0)

    def one_pair(pair, _):
        total_out[pair] = jnp.zeros((DIM, LANES), jnp.float32)
        stat[0:1, :] = jnp.full((1, LANES), FAR, jnp.float32)
        stat[1:2, :] = jnp.zeros((1, LANES), jnp.float32)

        def one_tile(tile, _):
            @pl.when(live[pair * TILES + tile] != 0)
            def _():
                keys = k_sorted[pl.ds(pl.multiple_of(tile * TILE, TILE), TILE), :]
                scores = dot(keys, q_sorted[pair], NT) * LOG2_SCALE
                mask = seen(key_ids, pair, tile, key_feature, query_feature, query_at)
                scores = jnp.where(jnp.concatenate([mask] * HEADS, axis=1), scores, FAR)
                old = stat[0:1, :]
                new = jnp.maximum(old, jnp.max(scores, axis=0, keepdims=True))
                terms = jnp.exp2(scores - new)
                fade = jnp.exp2(old - new)
                stat[0:1, :] = new
                stat[1:2, :] = stat[1:2, :] * fade + jnp.sum(terms, axis=0, keepdims=True)
                total_out[pair] = total_out[pair] * fade + dot(
                    v_turned[tile], terms.astype(jnp.bfloat16)
                )

            return 0

        lax.fori_loop(0, TILES, one_tile, 0)
        for h in range(HEADS):
            at = slice(h * PAIR, (h + 1) * PAIR)
            stat[2:3, at] = jnp.sum(
                flip(g_sorted[pair, at, :]) * total_out[pair, :, at], axis=0, keepdims=True
            )
        stat_out[pair] = stat[...]
        return 0

    lax.fori_loop(0, PAIRS, one_pair, 0)


def combine_kernel(query_rank, s0, s1, s2, s3, total, stat_out, o0, o1, o2, o3, rows):
    for pair in range(PAIRS):
        parts = [s[pair] for s in (s0, s1, s2, s3)]
        top = functools.reduce(jnp.maximum, [p[0:1, :] for p in parts])
        fades = [jnp.exp2(p[0:1, :] - top) for p in parts]
        mass = sum(p[1:2, :] * f for p, f in zip(parts, fades))
        lean = sum(p[2:3, :] * f for p, f in zip(parts, fades))
        stat_out[pair, 0:1, :] = top + jnp.log2(mass)
        stat_out[pair, 1:2, :] = lean / mass
        scaled = total[pair] * (fades[0] / mass)
        for h in range(HEADS):
            rows[pair, :, h * DIM:(h + 1) * DIM] = flip(scaled[:, h * PAIR:(h + 1) * PAIR]).astype(
                jnp.bfloat16
            )
    give_back(query_rank, rows, (o0, o1, o2, o3))


def give_back(query_rank, rows, outs):
    for r, out in enumerate(outs):
        for s in range(2):
            rank = query_rank[2 * r + s]
            at = pl.ds(pl.multiple_of(lax.rem(rank, 2) * SPAN, SPAN), SPAN)
            out[s * SPAN:(s + 1) * SPAN, :] = rows[rank // 2, at, :]


def backward_kernel(
    live, key_ids, key_rank, query_rank,
    q_sorted, g_sorted, k_sorted, v_sorted, key_feature, query_feature, query_at, stat,
    d0, d1, d2, d3, kv0, kv1,
    k_turned, key_total, value_total, query_total, rows,
):
    def turn(t, _):
        at = pl.ds(pl.multiple_of(t * TILE, TILE), TILE)
        k_turned[t] = flip(k_sorted[at, :]).astype(jnp.bfloat16)
        return 0

    lax.fori_loop(0, TILES, turn, 0)
    query_total[...] = jnp.zeros_like(query_total)

    def one_tile(tile, _):
        at = pl.ds(pl.multiple_of(tile * TILE, TILE), TILE)
        key_total[at, :] = jnp.zeros((TILE, DIM), jnp.float32)
        value_total[at, :] = jnp.zeros((TILE, DIM), jnp.float32)

        def one_pair(pair, _):
            @pl.when(live[pair * TILES + tile] != 0)
            def _():
                scores = dot(k_sorted[at, :], q_sorted[pair], NT) * LOG2_SCALE - stat[pair, 0:1, :]
                mask = seen(key_ids, pair, tile, key_feature, query_feature, query_at)
                scores = jnp.where(jnp.concatenate([mask] * HEADS, axis=1), scores, FAR)
                probs = jnp.exp2(scores)
                value_total[at, :] += dot(probs.astype(jnp.bfloat16), g_sorted[pair])
                prob_grad = dot(v_sorted[at, :], g_sorted[pair], NT)
                dscore = (probs * (prob_grad - stat[pair, 1:2, :])).astype(jnp.bfloat16)
                key_total[at, :] += dot(dscore, q_sorted[pair])
                query_total[pair] += dot(k_turned[tile], dscore)

            return 0

        lax.fori_loop(0, PAIRS, one_pair, 0)
        return 0

    lax.fori_loop(0, TILES, one_tile, 0)

    def unsort_keys(i, _):
        for c, kv in enumerate((kv0, kv1)):
            for s in range(2):
                rank = key_rank[c * KEY_SPANS // 2 + 2 * i + s]
                at = pl.ds(pl.multiple_of(rank * SPAN, SPAN), SPAN)
                both = jnp.concatenate([key_total[at, :] * SCALE, value_total[at, :]], axis=1)
                kv[i, s * SPAN:(s + 1) * SPAN, :] = both.astype(jnp.bfloat16)
        return 0

    lax.fori_loop(0, PLANE, unsort_keys, 0)
    for pair in range(PAIRS):
        for h in range(HEADS):
            turned = flip(query_total[pair, :, h * PAIR:(h + 1) * PAIR]) * SCALE
            rows[pair, :, h * DIM:(h + 1) * DIM] = turned.astype(jnp.bfloat16)
    give_back(query_rank, rows, (d0, d1, d2, d3))


def shape(dims, dtype):
    return jax.ShapeDtypeStruct(dims, dtype)


SMEM = pl.BlockSpec(memory_space=pltpu.SMEM)
VMEM = pl.BlockSpec(memory_space=pltpu.VMEM)
LIMIT = pltpu.CompilerParams(vmem_limit_bytes=48 * 1024 * 1024)


def ring(step):
    return [(i, i - i % SIDE + (i + step) % SIDE) for i in range(SIDE**3)]


def plan(mask_ranges, span_ids, place):
    line, z, core = place // SIDE, place % SIDE, lax.axis_index("grp")
    ids = span_ids.reshape(PLANE, SIDE, 2, 2)
    query_ids = jnp.concatenate([ids[line, (z - step) % SIDE, core] for step in SHIFTS])
    mine = ids[:, z]
    key_ids = jnp.stack([mine[:, core], mine[:, 1 - core]]).reshape(KEY_SPANS)

    def ranked(values):
        rank = jnp.sum((values[None, :] < values[:, None]).astype(jnp.int32), axis=1)
        at = jnp.arange(values.shape[0], dtype=jnp.int32)
        hit = (rank[:, None] == at[None, :]).astype(jnp.int32)
        return rank, jnp.sum(hit * values[:, None], axis=0)

    query_rank, query_sorted = ranked(query_ids)
    key_rank, key_sorted = ranked(key_ids)
    q_from, q_to, k_from, k_to, kind = [mask_ranges[:, column] for column in range(5)]
    within = jnp.arange(SPAN, dtype=jnp.int32)
    query_at = (query_sorted[:, None] * SPAN + within).reshape(PAIRS, 1, PAIR)
    key_at = (key_sorted[:, None] * SPAN + within).reshape(KEYS, 1)
    weight = jnp.where(kind == 1, 64.0, 1.0)
    query_feature = jnp.where(
        (query_at >= q_from[None, :, None]) & (query_at < q_to[None, :, None]),
        weight[None, :, None], 0.0,
    ).astype(jnp.bfloat16)
    query_feature = jnp.pad(query_feature, ((0, 0), (0, 16 - kind.shape[0]), (0, 0)))
    key_feature = ((key_at >= k_from[None, :]) & (key_at < k_to[None, :])).astype(jnp.bfloat16)
    key_feature = jnp.pad(key_feature, ((0, 0), (0, 16 - kind.shape[0])))
    q_low = jnp.maximum(query_sorted[:, None] * SPAN, q_from)
    q_high = jnp.minimum(query_sorted[:, None] * SPAN + SPAN, q_to)
    k_low = jnp.maximum(key_sorted[:, None] * SPAN, k_from)
    k_high = jnp.minimum(key_sorted[:, None] * SPAN + SPAN, k_to)
    some = (q_low < q_high)[:, None, :] & (k_low < k_high)[None, :, :]
    some = some & ((kind == 1) | (k_low[None, :, :] < q_high[:, None, :]))
    live = jnp.any(
        some.reshape(PAIRS, 2, TILES, TILE_SPANS, kind.shape[0]), axis=(1, 3, 4)
    ).astype(jnp.int32).reshape(PAIRS * TILES)
    query_at = jnp.broadcast_to(query_at, (PAIRS, 8, PAIR))
    return live, key_sorted, key_rank, query_rank, key_feature, query_feature, query_at


def per_device(queries, attn_keys, attn_values, out_grad, mask_ranges, span_ids):
    bf16, f32 = jnp.bfloat16, jnp.float32
    place = lax.axis_index("cp")
    planes = [[i * SIDE + z for i in range(PLANE)] for z in range(SIDE)]
    swap = [(0, 1), (1, 0)]

    q_parts = [queries] + [lax.ppermute(queries, "cp", ring(step)) for step in SHIFTS[1:]]
    g_parts = [out_grad] + [lax.ppermute(out_grad, "cp", ring(step)) for step in SHIFTS[1:]]
    both = jnp.concatenate([attn_keys, attn_values], axis=1)
    kv_mine = lax.all_to_all(
        jnp.broadcast_to(both[None], (PLANE, PAIR, 2 * DIM)), "cp", 0, 0, axis_index_groups=planes
    )
    kv_other = lax.ppermute(kv_mine, "grp", swap)
    live, key_ids, key_rank, query_rank, key_feature, query_feature, query_at = plan(
        mask_ranges, span_ids, place
    )

    total, stat, q_sorted, g_sorted, k_sorted, v_sorted = pl.pallas_call(
        forward_kernel,
        out_shape=(
            shape((PAIRS, DIM, LANES), f32),
            shape((PAIRS, 8, LANES), f32),
            shape((PAIRS, LANES, DIM), bf16),
            shape((PAIRS, LANES, DIM), bf16),
            shape((KEYS, DIM), bf16),
            shape((KEYS, DIM), bf16),
        ),
        in_specs=[SMEM] * 4 + [VMEM] * 13,
        out_specs=(VMEM,) * 6,
        scratch_shapes=[pltpu.VMEM((TILES, DIM, TILE), bf16), pltpu.VMEM((8, LANES), f32)],
        compiler_params=LIMIT,
        name="forward",
    )(
        live, key_ids, key_rank, query_rank, *q_parts, *g_parts, kv_mine, kv_other,
        key_feature, query_feature, query_at,
    )

    stats = [stat] + [lax.ppermute(stat, "cp", ring(step)) for step in SHIFTS[1:]]
    stat_all, *out_parts = pl.pallas_call(
        combine_kernel,
        out_shape=(shape((PAIRS, 8, LANES), f32),) + (shape((PAIR, HEADS * DIM), bf16),) * 4,
        in_specs=[SMEM] + [VMEM] * 5,
        out_specs=(VMEM,) * 5,
        scratch_shapes=[pltpu.VMEM((PAIRS, PAIR, HEADS * DIM), bf16)],
        compiler_params=LIMIT,
        name="combine",
    )(query_rank, *stats, total)

    def bring_home(parts):
        home = [parts[0]] + [
            lax.ppermute(part, "cp", ring(-step)) for part, step in zip(parts[1:], SHIFTS[1:])
        ]
        return sum(part.astype(f32) for part in home).astype(bf16)

    attn_out = bring_home(out_parts)

    *grad_parts, kv_grad_mine, kv_grad_other = pl.pallas_call(
        backward_kernel,
        out_shape=(shape((PAIR, HEADS * DIM), bf16),) * 4
        + (shape((PLANE, PAIR, 2 * DIM), bf16),) * 2,
        in_specs=[SMEM] * 4 + [VMEM] * 8,
        out_specs=(VMEM,) * 6,
        scratch_shapes=[
            pltpu.VMEM((TILES, DIM, TILE), bf16),
            pltpu.VMEM((KEYS, DIM), f32),
            pltpu.VMEM((KEYS, DIM), f32),
            pltpu.VMEM((PAIRS, DIM, LANES), f32),
            pltpu.VMEM((PAIRS, PAIR, HEADS * DIM), bf16),
        ],
        compiler_params=LIMIT,
        name="backward",
    )(
        live, key_ids, key_rank, query_rank, q_sorted, g_sorted, k_sorted, v_sorted,
        key_feature, query_feature, query_at, stat_all,
    )
    query_grad = bring_home(grad_parts)
    kv_other_core = lax.ppermute(kv_grad_other, "grp", swap)
    kv_sum = (kv_grad_mine.astype(f32) + kv_other_core.astype(f32)).astype(bf16)
    kv_terms = lax.all_to_all(kv_sum, "cp", 0, 0, axis_index_groups=planes)
    kv_grad = jnp.sum(kv_terms.astype(f32), axis=0).astype(bf16)
    return attn_out, query_grad, kv_grad[:, :DIM], kv_grad[:, DIM:]


def solution(mesh):
    rows = P(("cp", "grp"), None)
    return jax.shard_map(
        per_device,
        mesh=mesh,
        in_specs=(rows, rows, rows, rows, P(), P()),
        out_specs=(rows, rows, rows, rows),
        check_vma=False,
    )
```

```python
import functools
import math

import jax
import jax.numpy as jnp
from jax import lax
from jax.experimental import pallas as pl
from jax.experimental.pallas import tpu as pltpu
from jax.sharding import PartitionSpec as P

SIDE = 4
SPAN = 64
HEADS = 5
DIM = 128
PAIR = 2 * SPAN
LANES = HEADS * PAIR
PAIRS = SIDE
TILE = 256
TILE_SPANS = TILE // SPAN
PLANE = SIDE * SIDE
KEYS = 2 * PLANE * PAIR
KEY_SPANS = KEYS // SPAN
TILES = KEYS // TILE
FAR = -1e30
SCALE = 1.0 / math.sqrt(DIM)
LOG2_SCALE = SCALE * math.log2(math.e)
SHIFTS = (0, 1, -1, 2)
NT = (((1,), (1,)), ((), ()))
NN = (((1,), (0,)), ((), ()))


def dot(a, b, dims=NN):
    return lax.dot_general(a, b, dims, preferred_element_type=jnp.float32)


def flip(a):
    return jnp.transpose(a.astype(jnp.float32))


def rows_of(tile):
    return pl.ds(pl.multiple_of(tile * TILE, TILE), TILE)


def seen(key_ids, pair, tile, key_feature, query_feature, query_at):
    cover = dot(key_feature[rows_of(tile), :], query_feature[pair])
    row = lax.broadcasted_iota(jnp.int32, (SPAN, PAIR), 0)
    at = query_at[pair][0:1, :]
    past = jnp.concatenate(
        [row <= at - key_ids[tile * TILE_SPANS + s] * SPAN for s in range(TILE_SPANS)], axis=0
    )
    return cover > jnp.where(past, 0.5, 63.5)


def walk(order, counts, pair, step):
    whole, some = counts[2 * pair] // 2, counts[2 * pair + 1]

    def at(masked):
        def body(i, _):
            step(masked, order[pair * TILES + 2 * i], order[pair * TILES + 2 * i + 1])
            return 0

        return body

    lax.fori_loop(0, whole, at(False), 0)
    lax.fori_loop(whole, (some + 1) // 2, at(True), 0)


def forward_kernel(
    order, counts, key_ids, key_rank, query_rank,
    qg0, qg1, qg2, qg3, kv0, kv1, key_feature, query_feature, query_at,
    total_out, stat_out, q_sorted, g_sorted, k_sorted, v_sorted,
    v_turned, stat,
):
    for r, qg in enumerate((qg0, qg1, qg2, qg3)):
        for s in range(2):
            rank = query_rank[2 * r + s]
            pair, half = rank // 2, lax.rem(rank, 2)
            for h in range(HEADS):
                to = pl.ds(pl.multiple_of(h * PAIR + half * SPAN, SPAN), SPAN)
                q_at, g_at = h * DIM, (HEADS + h) * DIM
                q_sorted[pair, to, :] = qg[s * SPAN:(s + 1) * SPAN, q_at:q_at + DIM]
                g_sorted[pair, to, :] = qg[s * SPAN:(s + 1) * SPAN, g_at:g_at + DIM]

    def sort_keys(i, _):
        for c, kv in enumerate((kv0, kv1)):
            for s in range(2):
                rank = key_rank[c * KEY_SPANS // 2 + 2 * i + s]
                to = pl.ds(pl.multiple_of(rank * SPAN, SPAN), SPAN)
                rows = kv[i][s * SPAN:(s + 1) * SPAN, :]
                k_sorted[to, :] = rows[:, :DIM]
                v_sorted[to, :] = rows[:, DIM:]
        return 0

    lax.fori_loop(0, PLANE, sort_keys, 0)

    def turn(t, _):
        at = pl.ds(pl.multiple_of(t * TILE, TILE), TILE)
        v_turned[t] = flip(v_sorted[at, :]).astype(jnp.bfloat16)
        return 0

    lax.fori_loop(0, TILES, turn, 0)

    def one_pair(pair, _):
        total_out[pair] = jnp.zeros((DIM, LANES), jnp.float32)
        stat[0:1, :] = jnp.full((1, LANES), FAR, jnp.float32)
        stat[1:2, :] = jnp.zeros((1, LANES), jnp.float32)

        def step(masked, *tiles):
            scores = [
                dot(k_sorted[rows_of(tile), :], q_sorted[pair], NT) * LOG2_SCALE for tile in tiles
            ]
            if masked:
                masks = [
                    seen(key_ids, pair, tile, key_feature, query_feature, query_at)
                    for tile in tiles
                ]
                scores = [
                    jnp.where(jnp.concatenate([mask] * HEADS, axis=1), score, FAR)
                    for mask, score in zip(masks, scores)
                ]
            old = stat[0:1, :]
            new = old
            for score in scores:
                new = jnp.maximum(new, jnp.max(score, axis=0, keepdims=True))
            terms = [jnp.exp2(score - new) for score in scores]
            fade = jnp.exp2(old - new)
            stat[0:1, :] = new
            stat[1:2, :] = stat[1:2, :] * fade + sum(
                jnp.sum(term, axis=0, keepdims=True) for term in terms
            )
            total_out[pair] = total_out[pair] * fade + sum(
                dot(v_turned[tile], term.astype(jnp.bfloat16)) for tile, term in zip(tiles, terms)
            )

        walk(order, counts, pair, step)
        for h in range(HEADS):
            at = slice(h * PAIR, (h + 1) * PAIR)
            stat[2:3, at] = jnp.sum(
                flip(g_sorted[pair, at, :]) * total_out[pair, :, at], axis=0, keepdims=True
            )
        stat_out[pair] = stat[...]
        return 0

    lax.fori_loop(0, PAIRS, one_pair, 0)


def combine_kernel(query_rank, s0, s1, s2, s3, total, stat_out, o0, o1, o2, o3, rows):
    for pair in range(PAIRS):
        parts = [s[pair] for s in (s0, s1, s2, s3)]
        top = functools.reduce(jnp.maximum, [p[0:1, :] for p in parts])
        fades = [jnp.exp2(p[0:1, :] - top) for p in parts]
        mass = sum(p[1:2, :] * f for p, f in zip(parts, fades))
        lean = sum(p[2:3, :] * f for p, f in zip(parts, fades))
        stat_out[pair, 0:1, :] = top + jnp.log2(mass)
        stat_out[pair, 1:2, :] = lean / mass
        scaled = total[pair] * (fades[0] / mass)
        for h in range(HEADS):
            rows[pair, :, h * DIM:(h + 1) * DIM] = flip(scaled[:, h * PAIR:(h + 1) * PAIR]).astype(
                jnp.bfloat16
            )
    give_back(query_rank, rows, (o0, o1, o2, o3))


def give_back(query_rank, rows, outs):
    for r, out in enumerate(outs):
        for s in range(2):
            rank = query_rank[2 * r + s]
            at = pl.ds(pl.multiple_of(lax.rem(rank, 2) * SPAN, SPAN), SPAN)
            out[s * SPAN:(s + 1) * SPAN, :] = rows[rank // 2, at, :]


def backward_kernel(
    order, counts, key_ids, key_rank, query_rank,
    q_sorted, g_sorted, k_sorted, v_sorted, key_feature, query_feature, query_at, stat,
    d0, d1, d2, d3, kv0, kv1,
    k_turned, key_total, value_total, query_total, rows,
):
    def turn(t, _):
        at = pl.ds(pl.multiple_of(t * TILE, TILE), TILE)
        k_turned[t] = flip(k_sorted[at, :]).astype(jnp.bfloat16)
        return 0

    lax.fori_loop(0, TILES, turn, 0)
    query_total[...] = jnp.zeros_like(query_total)
    key_total[...] = jnp.zeros_like(key_total)
    value_total[...] = jnp.zeros_like(value_total)

    def one_pair(pair, _):
        def step(masked, *tiles):
            grown = []
            for tile in tiles:
                at = rows_of(tile)
                scores = dot(k_sorted[at, :], q_sorted[pair], NT) * LOG2_SCALE - stat[pair, 0:1, :]
                if masked:
                    mask = seen(key_ids, pair, tile, key_feature, query_feature, query_at)
                    scores = jnp.where(jnp.concatenate([mask] * HEADS, axis=1), scores, FAR)
                probs = jnp.exp2(scores)
                prob_grad = dot(v_sorted[at, :], g_sorted[pair], NT)
                dscore = (probs * (prob_grad - stat[pair, 1:2, :])).astype(jnp.bfloat16)
                grown.append(
                    (
                        dot(probs.astype(jnp.bfloat16), g_sorted[pair]),
                        dot(dscore, q_sorted[pair]),
                        dot(k_turned[tile], dscore),
                    )
                )
            for tile, (value_term, key_term, _) in zip(tiles, grown):
                value_total[rows_of(tile), :] += value_term
                key_total[rows_of(tile), :] += key_term
            query_total[pair] += sum(terms[2] for terms in grown)

        walk(order, counts, pair, step)
        return 0

    lax.fori_loop(0, PAIRS, one_pair, 0)

    def unsort_keys(i, _):
        for c, kv in enumerate((kv0, kv1)):
            for s in range(2):
                rank = key_rank[c * KEY_SPANS // 2 + 2 * i + s]
                at = pl.ds(pl.multiple_of(rank * SPAN, SPAN), SPAN)
                both = jnp.concatenate([key_total[at, :] * SCALE, value_total[at, :]], axis=1)
                kv[i, s * SPAN:(s + 1) * SPAN, :] = both.astype(jnp.bfloat16)
        return 0

    lax.fori_loop(0, PLANE, unsort_keys, 0)
    for pair in range(PAIRS):
        for h in range(HEADS):
            turned = flip(query_total[pair, :, h * PAIR:(h + 1) * PAIR]) * SCALE
            rows[pair, :, h * DIM:(h + 1) * DIM] = turned.astype(jnp.bfloat16)
    give_back(query_rank, rows, (d0, d1, d2, d3))


def shape(dims, dtype):
    return jax.ShapeDtypeStruct(dims, dtype)


def cost(matmuls):
    terms = PAIRS * LANES * KEYS // 2
    return pl.CostEstimate(
        flops=2 * matmuls * terms * DIM, bytes_accessed=8 * KEYS * DIM, transcendentals=terms
    )


SMEM = pl.BlockSpec(memory_space=pltpu.SMEM)
VMEM = pl.BlockSpec(memory_space=pltpu.VMEM)
LIMIT = pltpu.CompilerParams(vmem_limit_bytes=48 * 1024 * 1024)


def ring(step):
    return [(i, i - i % SIDE + (i + step) % SIDE) for i in range(SIDE**3)]


def plan(mask_ranges, span_ids, place):
    line, z, core = place // SIDE, place % SIDE, lax.axis_index("grp")
    ids = span_ids.reshape(PLANE, SIDE, 2, 2)
    query_ids = jnp.concatenate([ids[line, (z - step) % SIDE, core] for step in SHIFTS])
    mine = ids[:, z]
    key_ids = jnp.stack([mine[:, core], mine[:, 1 - core]]).reshape(KEY_SPANS)

    def ranked(values):
        rank = jnp.sum((values[None, :] < values[:, None]).astype(jnp.int32), axis=1)
        at = jnp.arange(values.shape[0], dtype=jnp.int32)
        hit = (rank[:, None] == at[None, :]).astype(jnp.int32)
        return rank, jnp.sum(hit * values[:, None], axis=0)

    query_rank, query_sorted = ranked(query_ids)
    key_rank, key_sorted = ranked(key_ids)
    q_from, q_to, k_from, k_to, kind = [mask_ranges[:, column] for column in range(5)]
    within = jnp.arange(SPAN, dtype=jnp.int32)
    query_at = (query_sorted[:, None] * SPAN + within).reshape(PAIRS, 1, PAIR)
    key_at = (key_sorted[:, None] * SPAN + within).reshape(KEYS, 1)
    weight = jnp.where(kind == 1, 64.0, 1.0)
    query_feature = jnp.where(
        (query_at >= q_from[None, :, None]) & (query_at < q_to[None, :, None]),
        weight[None, :, None], 0.0,
    ).astype(jnp.bfloat16)
    query_feature = jnp.pad(query_feature, ((0, 0), (0, 16 - kind.shape[0]), (0, 0)))
    key_feature = ((key_at >= k_from[None, :]) & (key_at < k_to[None, :])).astype(jnp.bfloat16)
    key_feature = jnp.pad(key_feature, ((0, 0), (0, 16 - kind.shape[0])))
    q_low = jnp.maximum(query_sorted[:, None] * SPAN, q_from)
    q_high = jnp.minimum(query_sorted[:, None] * SPAN + SPAN, q_to)
    k_low = jnp.maximum(key_sorted[:, None] * SPAN, k_from)
    k_high = jnp.minimum(key_sorted[:, None] * SPAN + SPAN, k_to)
    some = (q_low < q_high)[:, None, :] & (k_low < k_high)[None, :, :]
    some = some & ((kind == 1) | (k_low[None, :, :] < q_high[:, None, :]))
    whole = (
        (q_high - q_low == SPAN)[:, None, :]
        & (k_high - k_low == SPAN)[None, :, :]
        & ((kind == 1) | (k_high[None, :, :] <= q_low[:, None, :] + 1))
    )
    by_tile = (PAIRS, 2, TILES, TILE_SPANS)
    some = jnp.any(some, axis=2).reshape(by_tile).any(axis=(1, 3))
    whole = jnp.any(whole, axis=2).reshape(by_tile).all(axis=(1, 3))
    tile_at = jnp.arange(TILES, dtype=jnp.int32)
    key = jnp.where(whole, 0, jnp.where(some, TILES, 2 * TILES)) + tile_at
    rank = jnp.sum((key[:, None, :] < key[:, :, None]).astype(jnp.int32), axis=2)
    order = jnp.sum(
        jnp.where(rank[:, :, None] == tile_at, tile_at[:, None], 0), axis=1
    ).reshape(PAIRS * TILES)
    counts = jnp.stack(
        [jnp.sum(which.astype(jnp.int32), axis=1) for which in (whole, some)], axis=1
    ).reshape(2 * PAIRS)
    query_at = jnp.broadcast_to(query_at, (PAIRS, 8, PAIR))
    return order, counts, key_sorted, key_rank, query_rank, key_feature, query_feature, query_at


def per_device(queries, attn_keys, attn_values, out_grad, mask_ranges, span_ids):
    bf16, f32 = jnp.bfloat16, jnp.float32
    place = lax.axis_index("cp")
    planes = [[i * SIDE + z for i in range(PLANE)] for z in range(SIDE)]
    swap = [(0, 1), (1, 0)]

    both = jnp.concatenate([queries, out_grad], axis=1)
    qg_parts = [both] + [lax.ppermute(both, "cp", ring(step)) for step in SHIFTS[1:]]
    both = jnp.concatenate([attn_keys, attn_values], axis=1)
    kv_mine = lax.all_to_all(
        jnp.broadcast_to(both[None], (PLANE, PAIR, 2 * DIM)), "cp", 0, 0, axis_index_groups=planes
    )
    kv_other = lax.ppermute(kv_mine, "grp", swap)
    order, counts, key_ids, key_rank, query_rank, key_feature, query_feature, query_at = plan(
        mask_ranges, span_ids, place
    )

    total, stat, q_sorted, g_sorted, k_sorted, v_sorted = pl.pallas_call(
        forward_kernel,
        out_shape=(
            shape((PAIRS, DIM, LANES), f32),
            shape((PAIRS, 8, LANES), f32),
            shape((PAIRS, LANES, DIM), bf16),
            shape((PAIRS, LANES, DIM), bf16),
            shape((KEYS, DIM), bf16),
            shape((KEYS, DIM), bf16),
        ),
        in_specs=[SMEM] * 5 + [VMEM] * 9,
        out_specs=(VMEM,) * 6,
        scratch_shapes=[pltpu.VMEM((TILES, DIM, TILE), bf16), pltpu.VMEM((8, LANES), f32)],
        compiler_params=LIMIT,
        cost_estimate=cost(2),
        name="forward",
    )(
        order, counts, key_ids, key_rank, query_rank, *qg_parts, kv_mine, kv_other,
        key_feature, query_feature, query_at,
    )

    stats = [stat] + [lax.ppermute(stat, "cp", ring(step)) for step in SHIFTS[1:]]
    stat_all, *out_parts = pl.pallas_call(
        combine_kernel,
        out_shape=(shape((PAIRS, 8, LANES), f32),) + (shape((PAIR, HEADS * DIM), bf16),) * 4,
        in_specs=[SMEM] + [VMEM] * 5,
        out_specs=(VMEM,) * 5,
        scratch_shapes=[pltpu.VMEM((PAIRS, PAIR, HEADS * DIM), bf16)],
        compiler_params=LIMIT,
        name="combine",
    )(query_rank, *stats, total)

    def bring_home(parts):
        home = [parts[0]] + [
            lax.ppermute(part, "cp", ring(-step)) for part, step in zip(parts[1:], SHIFTS[1:])
        ]
        return sum(part.astype(f32) for part in home).astype(bf16)

    attn_out = bring_home(out_parts)

    *grad_parts, kv_grad_mine, kv_grad_other = pl.pallas_call(
        backward_kernel,
        out_shape=(shape((PAIR, HEADS * DIM), bf16),) * 4
        + (shape((PLANE, PAIR, 2 * DIM), bf16),) * 2,
        in_specs=[SMEM] * 5 + [VMEM] * 8,
        out_specs=(VMEM,) * 6,
        scratch_shapes=[
            pltpu.VMEM((TILES, DIM, TILE), bf16),
            pltpu.VMEM((KEYS, DIM), f32),
            pltpu.VMEM((KEYS, DIM), f32),
            pltpu.VMEM((PAIRS, DIM, LANES), f32),
            pltpu.VMEM((PAIRS, PAIR, HEADS * DIM), bf16),
        ],
        compiler_params=LIMIT,
        cost_estimate=cost(5),
        name="backward",
    )(
        order, counts, key_ids, key_rank, query_rank, q_sorted, g_sorted, k_sorted, v_sorted,
        key_feature, query_feature, query_at, stat_all,
    )
    query_grad = bring_home(grad_parts)
    kv_other_core = lax.ppermute(kv_grad_other, "grp", swap)
    kv_sum = (kv_grad_mine.astype(f32) + kv_other_core.astype(f32)).astype(bf16)
    kv_terms = lax.all_to_all(kv_sum, "cp", 0, 0, axis_index_groups=planes)
    kv_grad = jnp.sum(kv_terms.astype(f32), axis=0).astype(bf16)
    return attn_out, query_grad, kv_grad[:, :DIM], kv_grad[:, DIM:]


def solution(mesh):
    rows = P(("cp", "grp"), None)
    return jax.shard_map(
        per_device,
        mesh=mesh,
        in_specs=(rows, rows, rows, rows, P(), P()),
        out_specs=(rows, rows, rows, rows),
        check_vma=False,
    )
```

```python
import functools
import math

import jax
import jax.numpy as jnp
from jax import lax
from jax.experimental import pallas as pl
from jax.experimental.pallas import tpu as pltpu
from jax.sharding import PartitionSpec as P

SIDE = 4
SPAN = 64
HEADS = 5
DIM = 128
PAIR = 2 * SPAN
LANES = HEADS * PAIR
PAIRS = 2 * SIDE
TILE = 128
TILE_SPANS = TILE // SPAN
PLANE = SIDE * SIDE
KEYS = PLANE * PAIR
KEY_SPANS = KEYS // SPAN
TILES = KEYS // TILE
STAT_ROWS = 3 * PAIRS
WIDTH = HEADS * DIM
FAR = -1e30
SCALE = 1.0 / math.sqrt(DIM)
LOG2_SCALE = SCALE * math.log2(math.e)
SHIFTS = (0, 1, -1, 2)
NN = (((1,), (0,)), ((), ()))
NT = (((1,), (1,)), ((), ()))


def dot(a, b, dims=NN):
    return lax.dot_general(a, b, dims, preferred_element_type=jnp.float32)


def flip(a):
    return jnp.transpose(a.astype(jnp.float32))


def rows_of(tile):
    return pl.ds(pl.multiple_of(tile * TILE, TILE), TILE)


def span_rows(ids, first, count, width):
    within = lax.broadcasted_iota(jnp.int32, (SPAN, width), 0)
    return jnp.concatenate([within + ids[first + s] * SPAN for s in range(count)], axis=0)


def seen(tile, key_ids, pair, ranges, query_feature, query_at):
    key_at = span_rows(key_ids, tile * TILE_SPANS, TILE_SPANS, PAIR)
    holds = (key_at >= ranges[0:1, :]) & (key_at < ranges[1:2, :])
    cover = dot(jnp.where(holds, 1.0, 0.0).astype(jnp.bfloat16), query_feature[pair])
    return cover > jnp.where(key_at <= query_at[pair, 0:1, :], 0.5, 63.5)


def set_features(query_ids, ranges, query_feature, query_at):
    for pair in range(PAIRS):
        at = span_rows(query_ids, 2 * pair, 2, PAIR)
        holds = (at >= ranges[2:3, :]) & (at < ranges[3:4, :])
        weight = jnp.where(ranges[4:5, :] == 1, 64.0, 1.0)
        query_feature[pair] = flip(jnp.where(holds, weight, 0.0)).astype(jnp.bfloat16)
        query_at[pair] = jnp.transpose(at)[0:8, :]


def walk(order, counts, pair, step):
    whole, some = counts[2 * pair], counts[2 * pair + 1]

    def run(masked, size, first, steps):
        def body(i, _):
            at = pair * TILES + first + i * size
            step(masked, [order[at + t] for t in range(size)])
            return 0

        lax.fori_loop(0, steps, body, 0)
        return first + steps * size

    done = run(False, 4, 0, whole // 4)
    done = run(True, 4, done, (some - done) // 4)
    run(True, 2, done, (some - done + 1) // 2)


def stack(ref, tiles):
    return jnp.concatenate([ref[rows_of(tile), :] for tile in tiles], axis=0)


def masks_of(tiles, *where):
    mask = jnp.concatenate([seen(tile, *where) for tile in tiles], axis=0)
    return jnp.concatenate([mask] * HEADS, axis=1)


def pack_kernel(queries, out_grad, keys, values, qg, kv, row, sems):
    copies = [
        pltpu.make_async_copy(keys, row.at[:, :DIM], sems.at[0]),
        pltpu.make_async_copy(values, row.at[:, DIM:], sems.at[1]),
        pltpu.make_async_copy(queries, qg.at[:, :WIDTH], sems.at[2]),
        pltpu.make_async_copy(out_grad, qg.at[:, WIDTH:], sems.at[3]),
    ]
    for copy in copies:
        copy.start()
    for copy in copies[:2]:
        copy.wait()
    for i in range(PLANE):
        kv[i] = row[...]
    for copy in copies[2:]:
        copy.wait()


def forward_kernel(
    order, counts, key_ids, key_rank, query_ids, query_rank,
    qg0, qg1, qg2, qg3, qg_other, kv, ranges,
    total_out, stat_out, q_sorted, g_sorted, k_sorted, v_sorted,
    v_turned, stat, query_feature, query_at,
):
    set_features(query_ids, ranges, query_feature, query_at)
    for r, qg in enumerate([qg0, qg1, qg2, qg3] + [qg_other.at[i] for i in range(SIDE)]):
        for s in range(2):
            rank = query_rank[2 * r + s]
            pair, half = rank // 2, lax.rem(rank, 2)
            for h in range(HEADS):
                to = pl.ds(pl.multiple_of(h * PAIR + half * SPAN, SPAN), SPAN)
                q_at, g_at = h * DIM, (HEADS + h) * DIM
                q_sorted[pair, to, :] = qg[s * SPAN:(s + 1) * SPAN, q_at:q_at + DIM]
                g_sorted[pair, to, :] = qg[s * SPAN:(s + 1) * SPAN, g_at:g_at + DIM]

    def sort_keys(i, _):
        for s in range(2):
            rank = key_rank[2 * i + s]
            to = pl.ds(pl.multiple_of(rank * SPAN, SPAN), SPAN)
            rows = kv[i, s * SPAN:(s + 1) * SPAN, :]
            k_sorted[to, :] = rows[:, :DIM]
            v_sorted[to, :] = rows[:, DIM:]
        return 0

    lax.fori_loop(0, PLANE, sort_keys, 0)
    for t in range(TILES):
        v_turned[t] = jnp.transpose(v_sorted[t * TILE:(t + 1) * TILE, :])

    def one_pair(pair, _):
        total_out[pair] = jnp.zeros((DIM, LANES), jnp.float32)
        stat[0:1, :] = jnp.full((1, LANES), FAR, jnp.float32)
        stat[1:2, :] = jnp.zeros((1, LANES), jnp.float32)

        def step(masked, tiles):
            scores = dot(stack(k_sorted, tiles), q_sorted[pair], NT) * LOG2_SCALE
            if masked:
                mask = masks_of(tiles, key_ids, pair, ranges, query_feature, query_at)
                scores = jnp.where(mask, scores, FAR)
            old = stat[0:1, :]
            new = jnp.maximum(old, jnp.max(scores, axis=0, keepdims=True))
            terms = jnp.exp2(scores - new)
            fade = jnp.exp2(old - new)
            stat[0:1, :] = new
            stat[1:2, :] = stat[1:2, :] * fade + jnp.sum(terms, axis=0, keepdims=True)
            values = jnp.concatenate([v_turned[tile] for tile in tiles], axis=1)
            total_out[pair] = total_out[pair] * fade + dot(values, terms.astype(jnp.bfloat16))

        walk(order, counts, pair, step)
        for h in range(HEADS):
            at = slice(h * PAIR, (h + 1) * PAIR)
            grad = jnp.transpose(g_sorted[pair, at, :]).astype(jnp.float32)
            stat[2:3, at] = jnp.sum(grad * total_out[pair, :, at], axis=0, keepdims=True)
        for kind in range(3):
            stat_out[pl.ds(kind * PAIRS + pair, 1), :] = stat[kind:kind + 1, :]
        return 0

    lax.fori_loop(0, PAIRS, one_pair, 0)


def merge(parts):
    tops, masses, leans = [[part[k * PAIRS:(k + 1) * PAIRS, :] for part in parts] for k in range(3)]
    top = functools.reduce(jnp.maximum, tops)
    fades = [jnp.exp2(one - top) for one in tops]
    mass = sum(one * fade for one, fade in zip(masses, fades))
    lean = sum(one * fade for one, fade in zip(leans, fades))
    return top, mass, lean


def merge_kernel(s0, s1, s2, s3, out):
    for kind, rows in enumerate(merge([s0, s1, s2, s3])):
        out[kind * PAIRS:(kind + 1) * PAIRS, :] = rows


def turn_kernel(k_sorted, k_turned):
    for t in range(TILES):
        k_turned[t] = jnp.transpose(k_sorted[t * TILE:(t + 1) * TILE, :])


def give_back(query_rank, rows, outs, column):
    for r, out in enumerate(outs):
        for s in range(2):
            rank = query_rank[2 * r + s]
            at = pl.ds(pl.multiple_of(lax.rem(rank, 2) * SPAN, SPAN), SPAN)
            out[s * SPAN:(s + 1) * SPAN, column:column + WIDTH] = rows[rank // 2, at, :]


def backward_kernel(
    order, counts, key_ids, key_rank, query_ids, query_rank,
    q_sorted, g_sorted, k_sorted, v_sorted, k_turned, ranges, stat_own, stat_mine, stat_other, total,
    od0, od1, od2, od3, od_other, kv,
    key_total, value_total, query_total, rows, stat, query_feature, query_at,
):
    set_features(query_ids, ranges, query_feature, query_at)
    outs = [od0, od1, od2, od3] + [od_other.at[i] for i in range(SIDE)]
    top, mass, lean = merge([stat_mine, stat_other])
    share = jnp.exp2(stat_own[0:PAIRS, :] - top) / mass
    top, lean = top + jnp.log2(mass), lean / mass
    for pair in range(PAIRS):
        stat[pair, 0:1, :] = top[pair:pair + 1, :]
        stat[pair, 1:2, :] = lean[pair:pair + 1, :]
        for h in range(HEADS):
            at = slice(h * PAIR, (h + 1) * PAIR)
            scaled = total[pair, :, at] * share[pair:pair + 1, at]
            rows[pair, :, h * DIM:(h + 1) * DIM] = flip(scaled).astype(jnp.bfloat16)
    give_back(query_rank, rows, outs, 0)

    query_total[...] = jnp.zeros_like(query_total)
    key_total[...] = jnp.zeros_like(key_total)
    value_total[...] = jnp.zeros_like(value_total)

    def one_pair(pair, _):
        def step(masked, tiles):
            scores = dot(stack(k_sorted, tiles), q_sorted[pair], NT) * LOG2_SCALE - stat[pair, 0:1, :]
            if masked:
                mask = masks_of(tiles, key_ids, pair, ranges, query_feature, query_at)
                scores = jnp.where(mask, scores, FAR)
            probs = jnp.exp2(scores)
            prob_grad = dot(stack(v_sorted, tiles), g_sorted[pair], NT)
            dscore = (probs * (prob_grad - stat[pair, 1:2, :])).astype(jnp.bfloat16)
            value_terms = dot(probs.astype(jnp.bfloat16), g_sorted[pair])
            key_terms = dot(dscore, q_sorted[pair])
            keys = jnp.concatenate([k_turned[tile] for tile in tiles], axis=1)
            query_total[pair] += dot(keys, dscore)
            for i, tile in enumerate(tiles):
                at = slice(i * TILE, (i + 1) * TILE)
                value_total[rows_of(tile), :] += value_terms[at]
                key_total[rows_of(tile), :] += key_terms[at]

        walk(order, counts, pair, step)
        return 0

    lax.fori_loop(0, PAIRS, one_pair, 0)

    def unsort_keys(i, _):
        for s in range(2):
            rank = key_rank[2 * i + s]
            at = pl.ds(pl.multiple_of(rank * SPAN, SPAN), SPAN)
            both = jnp.concatenate([key_total[at, :] * SCALE, value_total[at, :]], axis=1)
            kv[i, s * SPAN:(s + 1) * SPAN, :] = both.astype(jnp.bfloat16)
        return 0

    lax.fori_loop(0, PLANE, unsort_keys, 0)
    for pair in range(PAIRS):
        for h in range(HEADS):
            turned = flip(query_total[pair, :, h * PAIR:(h + 1) * PAIR]) * SCALE
            rows[pair, :, h * DIM:(h + 1) * DIM] = turned.astype(jnp.bfloat16)
    give_back(query_rank, rows, outs, WIDTH)


def shape(dims, dtype):
    return jax.ShapeDtypeStruct(dims, dtype)


def cost(matmuls):
    terms = PAIRS * LANES * KEYS // 2
    return pl.CostEstimate(
        flops=2 * matmuls * terms * DIM, bytes_accessed=8 * KEYS * DIM, transcendentals=terms
    )


SMEM = pl.BlockSpec(memory_space=pltpu.SMEM)
VMEM = pl.BlockSpec(memory_space=pltpu.VMEM)
HBM = pl.BlockSpec(memory_space=pltpu.HBM)


def ring(step):
    return [(i, i - i % SIDE + (i + step) % SIDE) for i in range(SIDE**3)]


def plan(mask_ranges, span_ids, place):
    line, z, core = place // SIDE, place % SIDE, lax.axis_index("grp")
    ids = span_ids.reshape(PLANE, SIDE, 2, 2)
    query_ids = jnp.concatenate(
        [ids[line, (z - step) % SIDE, side] for side in (core, 1 - core) for step in SHIFTS]
    )
    key_ids = ids[:, z, core].reshape(KEY_SPANS)

    def ranked(values):
        rank = jnp.sum((values[None, :] < values[:, None]).astype(jnp.int32), axis=1)
        at = jnp.arange(values.shape[0], dtype=jnp.int32)
        hit = (rank[:, None] == at[None, :]).astype(jnp.int32)
        return rank, jnp.sum(hit * values[:, None], axis=0)

    query_rank, query_sorted = ranked(query_ids)
    key_rank, key_sorted = ranked(key_ids)
    q_from, q_to, k_from, k_to, kind = [mask_ranges[:, column] for column in range(5)]
    q_low = jnp.maximum(query_sorted[:, None] * SPAN, q_from)
    q_high = jnp.minimum(query_sorted[:, None] * SPAN + SPAN, q_to)
    k_low = jnp.maximum(key_sorted[:, None] * SPAN, k_from)
    k_high = jnp.minimum(key_sorted[:, None] * SPAN + SPAN, k_to)
    some = (q_low < q_high)[:, None, :] & (k_low < k_high)[None, :, :]
    some = some & ((kind == 1) | (k_low[None, :, :] < q_high[:, None, :]))
    whole = (
        (q_high - q_low == SPAN)[:, None, :]
        & (k_high - k_low == SPAN)[None, :, :]
        & ((kind == 1) | (k_high[None, :, :] <= q_low[:, None, :] + 1))
    )
    by_tile = (PAIRS, 2, TILES, TILE_SPANS)
    some = jnp.any(some, axis=2).reshape(by_tile).any(axis=(1, 3))
    whole = jnp.any(whole, axis=2).reshape(by_tile).all(axis=(1, 3))
    tile_at = jnp.arange(TILES, dtype=jnp.int32)
    key = jnp.where(whole, 0, jnp.where(some, TILES, 2 * TILES)) + tile_at
    rank = jnp.sum((key[:, None, :] < key[:, :, None]).astype(jnp.int32), axis=2)
    order = jnp.sum(
        jnp.where(rank[:, :, None] == tile_at, tile_at[:, None], 0), axis=1
    ).reshape(PAIRS * TILES)
    counts = jnp.stack(
        [jnp.sum(which.astype(jnp.int32), axis=1) for which in (whole, some)], axis=1
    ).reshape(2 * PAIRS)
    columns = jnp.stack([k_from, k_to, q_from, q_to, kind])
    ranges = jnp.pad(columns, ((0, 3), (0, PAIR - kind.shape[0])))
    return order, counts, key_sorted, key_rank, query_sorted, query_rank, ranges


def kernel(body, name, scalars, operands, outs, scratch=(), matmuls=0, mebibytes=16, place=VMEM):
    return pl.pallas_call(
        body,
        out_shape=tuple(shape(*out) for out in outs),
        in_specs=[SMEM] * len(scalars) + [place] * len(operands),
        out_specs=(VMEM,) * len(outs),
        scratch_shapes=[pltpu.VMEM(*one) if isinstance(one, tuple) else one for one in scratch],
        compiler_params=pltpu.CompilerParams(vmem_limit_bytes=mebibytes * 1024 * 1024),
        cost_estimate=cost(matmuls) if matmuls else None,
        name=name,
    )(*scalars, *operands)


def per_device(queries, attn_keys, attn_values, out_grad, mask_ranges, span_ids):
    bf16, f32 = jnp.bfloat16, jnp.float32
    place = lax.axis_index("cp")
    planes = [[i * SIDE + z for i in range(PLANE)] for z in range(SIDE)]

    def swap(array):
        return lax.ppermute(array, "grp", [(0, 1), (1, 0)])

    def around(array, sign=1):
        return [lax.ppermute(array, "cp", ring(sign * step)) for step in SHIFTS[1:]]

    def plane_exchange(array):
        return lax.all_to_all(array, "cp", 0, 0, axis_index_groups=planes)

    sorted_shape = ((PAIRS, LANES, DIM), bf16)
    keys_shape = ((KEYS, DIM), bf16)
    kv_shape = ((PLANE, PAIR, 2 * DIM), bf16)
    line_shape = ((PAIR, 2 * WIDTH), bf16)
    lines_shape = ((SIDE, PAIR, 2 * WIDTH), bf16)
    tiles_shape = ((TILES, DIM, TILE), bf16)
    stat_shape = ((STAT_ROWS, LANES), f32)
    feature_shapes = [((PAIRS, PAIR, PAIR), bf16), ((PAIRS, 8, PAIR), jnp.int32)]

    qg, kv_copies = kernel(
        pack_kernel, "pack", [], [queries, out_grad, attn_keys, attn_values],
        [line_shape, kv_shape], [((PAIR, 2 * DIM), bf16), pltpu.SemaphoreType.DMA((4,))],
        mebibytes=60, place=HBM,
    )
    qg_parts = [qg] + around(qg)
    kv = plane_exchange(kv_copies)
    qg_other = swap(jnp.stack(qg_parts))
    order, counts, key_ids, key_rank, query_ids, query_rank, ranges = plan(
        mask_ranges, span_ids, place
    )
    lists = [order, counts, key_ids, key_rank, query_ids, query_rank]
    total, stat, q_sorted, g_sorted, k_sorted, v_sorted = kernel(
        forward_kernel, "forward", lists, [*qg_parts, qg_other, kv, ranges],
        [((PAIRS, DIM, LANES), f32), stat_shape, *[sorted_shape] * 2, *[keys_shape] * 2],
        [tiles_shape, ((8, LANES), f32), *feature_shapes],
        matmuls=2,
    )
    (k_turned,) = kernel(turn_kernel, "turn", [], [k_sorted], [tiles_shape])
    (stat_mine,) = kernel(merge_kernel, "merge", [], [stat, *around(stat)], [stat_shape])
    *home, od_other, kv_grad = kernel(
        backward_kernel, "backward", lists,
        [
            q_sorted, g_sorted, k_sorted, v_sorted, k_turned, ranges,
            stat, stat_mine, swap(stat_mine), total,
        ],
        [line_shape] * SIDE + [lines_shape, kv_shape],
        [
            *[((KEYS, DIM), f32)] * 2, ((PAIRS, DIM, LANES), f32), ((PAIRS, PAIR, WIDTH), bf16),
            ((PAIRS, 8, LANES), f32), *feature_shapes,
        ],
        matmuls=5, mebibytes=28,
    )
    kv_terms = plane_exchange(kv_grad)
    od_other = swap(od_other)
    home = [
        (part.astype(f32) + other.astype(f32)).astype(bf16) for part, other in zip(home, od_other)
    ]
    home[1:] = [
        lax.ppermute(part, "cp", ring(-step)) for part, step in zip(home[1:], SHIFTS[1:])
    ]
    out, query_grad = [
        sum(part[:, at:at + WIDTH].astype(f32) for part in home).astype(bf16) for at in (0, WIDTH)
    ]
    kv_sum = jnp.sum(kv_terms.astype(f32), axis=0).astype(bf16)
    return out, query_grad, kv_sum[:, :DIM], kv_sum[:, DIM:]


def solution(mesh):
    rows = P(("cp", "grp"), None)
    return jax.shard_map(
        per_device,
        mesh=mesh,
        in_specs=(rows, rows, rows, rows, P(), P()),
        out_specs=(rows, rows, rows, rows),
        check_vma=False,
    )
```

```python
import functools
import math

import jax
import jax.numpy as jnp
from jax import lax
from jax.experimental import pallas as pl
from jax.experimental.pallas import tpu as pltpu
from jax.sharding import PartitionSpec as P

SIDE = 4
SPAN = 64
HEADS = 5
DIM = 128
PAIR = 2 * SPAN
LANES = HEADS * PAIR
PAIRS = 2 * SIDE
TILE = 128
TILE_SPANS = TILE // SPAN
PLANE = SIDE * SIDE
KEYS = PLANE * PAIR
KEY_SPANS = KEYS // SPAN
TILES = KEYS // TILE
STAT_ROWS = 2 * PAIRS
WIDTH = HEADS * DIM
GROUPS = (slice(0, 256), slice(256, 512), slice(512, 640))
FAR = -1e30
SCALE = 1.0 / math.sqrt(DIM)
LOG2_SCALE = SCALE * math.log2(math.e)
SHIFTS = (0, 1, -1, 2)
NN = (((1,), (0,)), ((), ()))
NT = (((1,), (1,)), ((), ()))


def dot(a, b, dims=NN):
    return lax.dot_general(a, b, dims, preferred_element_type=jnp.float32)


def flip(a):
    return jnp.transpose(a.astype(jnp.float32))


def rows_of(tile):
    return pl.ds(pl.multiple_of(tile * TILE, TILE), TILE)


def span_rows(ids, first, count, width):
    within = lax.broadcasted_iota(jnp.int32, (SPAN, width), 0)
    return jnp.concatenate([within + ids[first + s] * SPAN for s in range(count)], axis=0)


def seen(tile, key_ids, pair, ranges, query_feature, query_at):
    key_at = span_rows(key_ids, tile * TILE_SPANS, TILE_SPANS, PAIR)
    holds = (key_at >= ranges[0:1, :]) & (key_at < ranges[1:2, :])
    cover = dot(jnp.where(holds, 1.0, 0.0).astype(jnp.bfloat16), query_feature[pair])
    seen = cover > jnp.where(key_at <= query_at[pair, 0:1, :], 0.5, 63.5)
    return jnp.where(seen, 0.0, FAR)


def set_features(query_ids, ranges, query_feature, query_at):
    for pair in range(PAIRS):
        at = span_rows(query_ids, 2 * pair, 2, PAIR)
        holds = (at >= ranges[2:3, :]) & (at < ranges[3:4, :])
        weight = jnp.where(ranges[4:5, :] == 1, 64.0, 1.0)
        query_feature[pair] = flip(jnp.where(holds, weight, 0.0)).astype(jnp.bfloat16)
        query_at[pair] = jnp.transpose(at)[0:8, :]


def walk(order, counts, pair, step):
    whole, some = counts[2 * pair], counts[2 * pair + 1]

    def run(masked, size, first, steps):
        def body(i, _):
            at = pair * TILES + first + i * size
            step(masked, [order[at + t] for t in range(size)])
            return 0

        lax.fori_loop(0, steps, body, 0)
        return first + steps * size

    done = run(False, 4, 0, whole // 4)
    done = run(True, 4, done, (some - done) // 4)
    for size in (3, 2, 1):
        run(True, size, done, jnp.where(some - done == size, 1, 0))


def stack(ref, tiles):
    return jnp.concatenate([ref[rows_of(tile), :] for tile in tiles], axis=0)


def mask_of(tiles, *where):
    return jnp.concatenate([seen(tile, *where) for tile in tiles], axis=0)


def hide(mask, scores, heads):
    return scores + jnp.concatenate([mask] * heads, axis=1)


def pack_kernel(queries, out_grad, keys, values, qg, kv, row, sems):
    copies = [
        pltpu.make_async_copy(keys, row.at[:, :DIM], sems.at[0]),
        pltpu.make_async_copy(values, row.at[:, DIM:], sems.at[1]),
        pltpu.make_async_copy(queries, qg.at[:, :WIDTH], sems.at[2]),
        pltpu.make_async_copy(out_grad, qg.at[:, WIDTH:], sems.at[3]),
    ]
    for copy in copies:
        copy.start()
    for copy in copies[:2]:
        copy.wait()
    for i in range(PLANE):
        kv[i] = row[...]
    for copy in copies[2:]:
        copy.wait()


def join_kernel(a0, a1, a2, a3, b, c0, c1, c2, c3):
    for i, (a, c) in enumerate(zip((a0, a1, a2, a3), (c0, c1, c2, c3))):
        c[...] = (a[...].astype(jnp.float32) + b[i].astype(jnp.float32)).astype(jnp.bfloat16)


def forward_kernel(
    order, counts, key_ids, key_rank, query_ids, query_rank,
    qg0, qg1, qg2, qg3, qg4, qg5, qg6, qg7, kv, ranges,
    total_out, top_out, stat_out, q_sorted, g_sorted, k_sorted, v_sorted,
    v_turned, stat, query_feature, query_at,
):
    set_features(query_ids, ranges, query_feature, query_at)
    for r, qg in enumerate((qg0, qg1, qg2, qg3, qg4, qg5, qg6, qg7)):
        for s in range(2):
            rank = query_rank[2 * r + s]
            pair, half = rank // 2, lax.rem(rank, 2)
            for h in range(HEADS):
                to = pl.ds(pl.multiple_of(h * PAIR + half * SPAN, SPAN), SPAN)
                q_at, g_at = h * DIM, (HEADS + h) * DIM
                q_sorted[pair, to, :] = qg[s * SPAN:(s + 1) * SPAN, q_at:q_at + DIM]
                g_sorted[pair, to, :] = qg[s * SPAN:(s + 1) * SPAN, g_at:g_at + DIM]

    def sort_keys(i, _):
        for s in range(2):
            rank = key_rank[2 * i + s]
            to = pl.ds(pl.multiple_of(rank * SPAN, SPAN), SPAN)
            rows = kv[i, s * SPAN:(s + 1) * SPAN, :]
            k_sorted[to, :] = rows[:, :DIM]
            v_sorted[to, :] = rows[:, DIM:]
        return 0

    lax.fori_loop(0, PLANE, sort_keys, 0)
    for t in range(TILES):
        v_turned[t] = jnp.transpose(v_sorted[t * TILE:(t + 1) * TILE, :])

    def one_pair(pair, _):
        total_out[pair] = jnp.zeros((DIM, LANES), jnp.float32)
        stat[0:1, :] = jnp.full((1, LANES), FAR, jnp.float32)
        stat[1:2, :] = jnp.zeros((1, LANES), jnp.float32)

        def step(masked, tiles):
            keys = stack(k_sorted, tiles)
            values = jnp.concatenate([v_turned[tile] for tile in tiles], axis=1)
            if masked:
                mask = mask_of(tiles, key_ids, pair, ranges, query_feature, query_at)
            raw = dot(keys, q_sorted[pair, GROUPS[0], :], NT)
            for i, group in enumerate(GROUPS):
                scores = raw * LOG2_SCALE
                if i + 1 < len(GROUPS):
                    raw = dot(keys, q_sorted[pair, GROUPS[i + 1], :], NT)
                if masked:
                    scores = hide(mask, scores, (group.stop - group.start) // PAIR)
                old = stat[0:1, group]
                new = jnp.maximum(old, jnp.max(scores, axis=0, keepdims=True))
                terms = jnp.exp2(scores - new)
                fade = jnp.exp2(old - new)
                stat[0:1, group] = new
                stat[1:2, group] = stat[1:2, group] * fade + jnp.sum(terms, axis=0, keepdims=True)
                total_out[pair, :, group] = total_out[pair, :, group] * fade + dot(
                    values, terms.astype(jnp.bfloat16)
                )

        walk(order, counts, pair, step)
        for h in range(HEADS):
            at = slice(h * PAIR, (h + 1) * PAIR)
            grad = jnp.transpose(g_sorted[pair, at, :]).astype(jnp.float32)
            stat[2:3, at] = jnp.sum(grad * total_out[pair, :, at], axis=0, keepdims=True)
        top, mass = stat[0:1, :], jnp.maximum(stat[1:2, :], 1e-30)
        top_out[pl.ds(pair, 1), :] = top
        stat_out[pl.ds(pair, 1), :] = top + jnp.log2(mass)
        stat_out[pl.ds(PAIRS + pair, 1), :] = stat[2:3, :] / mass
        return 0

    lax.fori_loop(0, PAIRS, one_pair, 0)


def merge(parts):
    logs, leans = [[part[k * PAIRS:(k + 1) * PAIRS, :] for part in parts] for k in range(2)]
    top = functools.reduce(jnp.maximum, logs)
    masses = [jnp.exp2(one - top) for one in logs]
    mass = sum(masses)
    lean = sum(one * part for one, part in zip(leans, masses))
    return top + jnp.log2(mass), lean / mass


def merge_kernel(s0, s1, s2, s3, out):
    for kind, rows in enumerate(merge([s0, s1, s2, s3])):
        out[kind * PAIRS:(kind + 1) * PAIRS, :] = rows


def turn_kernel(k_sorted, k_turned):
    for t in range(TILES):
        k_turned[t] = jnp.transpose(k_sorted[t * TILE:(t + 1) * TILE, :])


def give_back(query_rank, rows, outs, column):
    for r, out in enumerate(outs):
        for s in range(2):
            rank = query_rank[2 * r + s]
            at = pl.ds(pl.multiple_of(lax.rem(rank, 2) * SPAN, SPAN), SPAN)
            out[s * SPAN:(s + 1) * SPAN, column:column + WIDTH] = rows[rank // 2, at, :]


def backward_kernel(
    order, counts, key_ids, key_rank, query_ids, query_rank,
    q_sorted, g_sorted, k_sorted, v_sorted, k_turned, ranges, top_own, stat_mine, stat_other, total,
    od0, od1, od2, od3, od_other, kv,
    key_total, value_total, query_total, rows, stat, query_feature, query_at,
):
    set_features(query_ids, ranges, query_feature, query_at)
    outs = [od0, od1, od2, od3] + [od_other.at[i] for i in range(SIDE)]
    log_total, lean = merge([stat_mine, stat_other])
    share = jnp.exp2(top_own[...] - log_total)
    for pair in range(PAIRS):
        stat[pair, 0:1, :] = log_total[pair:pair + 1, :]
        stat[pair, 1:2, :] = lean[pair:pair + 1, :]
        for h in range(HEADS):
            at = slice(h * PAIR, (h + 1) * PAIR)
            scaled = total[pair, :, at] * share[pair:pair + 1, at]
            rows[pair, :, h * DIM:(h + 1) * DIM] = flip(scaled).astype(jnp.bfloat16)
    give_back(query_rank, rows, outs, 0)

    query_total[...] = jnp.zeros_like(query_total)
    key_total[...] = jnp.zeros_like(key_total)
    value_total[...] = jnp.zeros_like(value_total)

    def one_pair(pair, _):
        def step(masked, tiles):
            keys, values = stack(k_sorted, tiles), stack(v_sorted, tiles)
            keys_turned = jnp.concatenate([k_turned[tile] for tile in tiles], axis=1)
            if masked:
                mask = mask_of(tiles, key_ids, pair, ranges, query_feature, query_at)

            def products(group):
                return (
                    dot(keys, q_sorted[pair, group, :], NT),
                    dot(values, g_sorted[pair, group, :], NT),
                )

            key_terms, value_terms = 0.0, 0.0
            raw, prob_grad = products(GROUPS[0])
            for i, group in enumerate(GROUPS):
                scores = raw * LOG2_SCALE - stat[pair, 0:1, group]
                lean = prob_grad - stat[pair, 1:2, group]
                if i + 1 < len(GROUPS):
                    raw, prob_grad = products(GROUPS[i + 1])
                if masked:
                    scores = hide(mask, scores, (group.stop - group.start) // PAIR)
                probs = jnp.exp2(scores)
                dscore = (probs * lean).astype(jnp.bfloat16)
                value_terms += dot(probs.astype(jnp.bfloat16), g_sorted[pair, group, :])
                key_terms += dot(dscore, q_sorted[pair, group, :])
                query_total[pair, :, group] += dot(keys_turned, dscore)
            for i, tile in enumerate(tiles):
                at = slice(i * TILE, (i + 1) * TILE)
                value_total[rows_of(tile), :] += value_terms[at]
                key_total[rows_of(tile), :] += key_terms[at]

        walk(order, counts, pair, step)
        return 0

    lax.fori_loop(0, PAIRS, one_pair, 0)

    def unsort_keys(i, _):
        for s in range(2):
            rank = key_rank[2 * i + s]
            at = pl.ds(pl.multiple_of(rank * SPAN, SPAN), SPAN)
            both = jnp.concatenate([key_total[at, :] * SCALE, value_total[at, :]], axis=1)
            kv[i, s * SPAN:(s + 1) * SPAN, :] = both.astype(jnp.bfloat16)
        return 0

    lax.fori_loop(0, PLANE, unsort_keys, 0)
    for pair in range(PAIRS):
        for h in range(HEADS):
            turned = flip(query_total[pair, :, h * PAIR:(h + 1) * PAIR]) * SCALE
            rows[pair, :, h * DIM:(h + 1) * DIM] = turned.astype(jnp.bfloat16)
    give_back(query_rank, rows, outs, WIDTH)


def shape(dims, dtype):
    return jax.ShapeDtypeStruct(dims, dtype)


def cost(matmuls):
    terms = PAIRS * LANES * KEYS // 2
    return pl.CostEstimate(
        flops=2 * matmuls * terms * DIM, bytes_accessed=8 * KEYS * DIM, transcendentals=terms
    )


SMEM = pl.BlockSpec(memory_space=pltpu.SMEM)
VMEM = pl.BlockSpec(memory_space=pltpu.VMEM)
HBM = pl.BlockSpec(memory_space=pltpu.HBM)


def ring(step):
    return [(i, i - i % SIDE + (i + step) % SIDE) for i in range(SIDE**3)]


def plan(mask_ranges, span_ids, place):
    line, z, core = place // SIDE, place % SIDE, lax.axis_index("grp")
    ids = span_ids.reshape(PLANE, SIDE, 2, 2)
    query_ids = jnp.concatenate(
        [ids[line, (z - step) % SIDE, side] for side in (core, 1 - core) for step in SHIFTS]
    )
    key_ids = ids[:, z, core].reshape(KEY_SPANS)

    def ranked(values):
        rank = jnp.sum((values[None, :] < values[:, None]).astype(jnp.int32), axis=1)
        at = jnp.arange(values.shape[0], dtype=jnp.int32)
        hit = (rank[:, None] == at[None, :]).astype(jnp.int32)
        return rank, jnp.sum(hit * values[:, None], axis=0)

    query_rank, query_sorted = ranked(query_ids)
    key_rank, key_sorted = ranked(key_ids)
    q_from, q_to, k_from, k_to, kind = [mask_ranges[:, column] for column in range(5)]
    q_low = jnp.maximum(query_sorted[:, None] * SPAN, q_from)
    q_high = jnp.minimum(query_sorted[:, None] * SPAN + SPAN, q_to)
    k_low = jnp.maximum(key_sorted[:, None] * SPAN, k_from)
    k_high = jnp.minimum(key_sorted[:, None] * SPAN + SPAN, k_to)
    some = (q_low < q_high)[:, None, :] & (k_low < k_high)[None, :, :]
    some = some & ((kind == 1) | (k_low[None, :, :] < q_high[:, None, :]))
    whole = (
        (q_high - q_low == SPAN)[:, None, :]
        & (k_high - k_low == SPAN)[None, :, :]
        & ((kind == 1) | (k_high[None, :, :] <= q_low[:, None, :] + 1))
    )
    by_tile = (PAIRS, 2, TILES, TILE_SPANS)
    some = jnp.any(some, axis=2).reshape(by_tile).any(axis=(1, 3))
    whole = jnp.any(whole, axis=2).reshape(by_tile).all(axis=(1, 3))
    tile_at = jnp.arange(TILES, dtype=jnp.int32)
    key = jnp.where(whole, 0, jnp.where(some, TILES, 2 * TILES)) + tile_at
    rank = jnp.sum((key[:, None, :] < key[:, :, None]).astype(jnp.int32), axis=2)
    order = jnp.sum(
        jnp.where(rank[:, :, None] == tile_at, tile_at[:, None], 0), axis=1
    ).reshape(PAIRS * TILES)
    counts = jnp.stack(
        [jnp.sum(which.astype(jnp.int32), axis=1) for which in (whole, some)], axis=1
    ).reshape(2 * PAIRS)
    columns = jnp.stack([k_from, k_to, q_from, q_to, kind])
    ranges = jnp.pad(columns, ((0, 3), (0, PAIR - kind.shape[0])))
    return order, counts, key_sorted, key_rank, query_sorted, query_rank, ranges


def kernel(body, name, scalars, operands, outs, scratch=(), matmuls=0, mebibytes=16, place=VMEM):
    return pl.pallas_call(
        body,
        out_shape=tuple(shape(*out) for out in outs),
        in_specs=[SMEM] * len(scalars) + [place] * len(operands),
        out_specs=(VMEM,) * len(outs),
        scratch_shapes=[pltpu.VMEM(*one) if isinstance(one, tuple) else one for one in scratch],
        compiler_params=pltpu.CompilerParams(vmem_limit_bytes=mebibytes * 1024 * 1024),
        cost_estimate=cost(matmuls) if matmuls else None,
        name=name,
    )(*scalars, *operands)


def per_device(queries, attn_keys, attn_values, out_grad, mask_ranges, span_ids):
    bf16, f32 = jnp.bfloat16, jnp.float32
    place = lax.axis_index("cp")
    planes = [[i * SIDE + z for i in range(PLANE)] for z in range(SIDE)]

    def swap(array):
        return lax.ppermute(array, "grp", [(0, 1), (1, 0)])

    def around(array, sign=1):
        return [lax.ppermute(array, "cp", ring(sign * step)) for step in SHIFTS[1:]]

    def plane_exchange(array):
        return lax.all_to_all(array, "cp", 0, 0, axis_index_groups=planes)

    sorted_shape = ((PAIRS, LANES, DIM), bf16)
    keys_shape = ((KEYS, DIM), bf16)
    kv_shape = ((PLANE, PAIR, 2 * DIM), bf16)
    line_shape = ((PAIR, 2 * WIDTH), bf16)
    lines_shape = ((SIDE, PAIR, 2 * WIDTH), bf16)
    tiles_shape = ((TILES, DIM, TILE), bf16)
    stat_shape = ((STAT_ROWS, LANES), f32)
    feature_shapes = [((PAIRS, PAIR, PAIR), bf16), ((PAIRS, 8, PAIR), jnp.int32)]

    qg, kv_copies = kernel(
        pack_kernel, "pack", [], [queries, out_grad, attn_keys, attn_values],
        [line_shape, kv_shape], [((PAIR, 2 * DIM), bf16), pltpu.SemaphoreType.DMA((4,))],
        mebibytes=60, place=HBM,
    )
    qg_parts = [qg] + around(qg)
    kv = plane_exchange(kv_copies)
    qg_parts += [swap(part) for part in qg_parts]
    order, counts, key_ids, key_rank, query_ids, query_rank, ranges = plan(
        mask_ranges, span_ids, place
    )
    lists = [order, counts, key_ids, key_rank, query_ids, query_rank]
    total, top, stat, q_sorted, g_sorted, k_sorted, v_sorted = kernel(
        forward_kernel, "forward", lists, [*qg_parts, kv, ranges],
        [((PAIRS, DIM, LANES), f32), ((PAIRS, LANES), f32), stat_shape, *[sorted_shape] * 2, *[keys_shape] * 2],
        [tiles_shape, ((8, LANES), f32), *feature_shapes],
        matmuls=2,
    )
    (k_turned,) = kernel(turn_kernel, "turn", [], [k_sorted], [tiles_shape])
    (stat_mine,) = kernel(merge_kernel, "merge", [], [stat, *around(stat)], [stat_shape])
    *home, od_other, kv_grad = kernel(
        backward_kernel, "backward", lists,
        [
            q_sorted, g_sorted, k_sorted, v_sorted, k_turned, ranges,
            top, stat_mine, swap(stat_mine), total,
        ],
        [line_shape] * SIDE + [lines_shape, kv_shape],
        [
            *[((KEYS, DIM), f32)] * 2, ((PAIRS, DIM, LANES), f32), ((PAIRS, PAIR, WIDTH), bf16),
            ((PAIRS, 8, LANES), f32), *feature_shapes,
        ],
        matmuls=5, mebibytes=28,
    )
    kv_terms = plane_exchange(kv_grad)
    od_other = swap(od_other)
    home = list(kernel(join_kernel, "join", [], [*home, od_other], [line_shape] * SIDE))
    home[1:] = [
        lax.ppermute(part, "cp", ring(-step)) for part, step in zip(home[1:], SHIFTS[1:])
    ]
    out, query_grad = [
        sum(part[:, at:at + WIDTH].astype(f32) for part in home).astype(bf16) for at in (0, WIDTH)
    ]
    kv_sum = jnp.sum(kv_terms.astype(f32), axis=0).astype(bf16)
    return out, query_grad, kv_sum[:, :DIM], kv_sum[:, DIM:]


def solution(mesh):
    rows = P(("cp", "grp"), None)
    return jax.shard_map(
        per_device,
        mesh=mesh,
        in_specs=(rows, rows, rows, rows, P(), P()),
        out_specs=(rows, rows, rows, rows),
        check_vma=False,
    )
```

```python
import functools
import math

import jax
import jax.numpy as jnp
from jax import lax
from jax.experimental import pallas as pl
from jax.experimental.pallas import tpu as pltpu
from jax.sharding import PartitionSpec as P

SIDE = 4
SPAN = 64
HEADS = 5
DIM = 128
PAIR = 2 * SPAN
LANES = HEADS * PAIR
PAIRS = 2 * SIDE
TILE = 128
TILE_SPANS = TILE // SPAN
PLANE = SIDE * SIDE
KEYS = PLANE * PAIR
KEY_SPANS = KEYS // SPAN
TILES = KEYS // TILE
STAT_ROWS = 2 * PAIRS
WIDTH = HEADS * DIM
GROUPS = (slice(0, 256), slice(256, 512), slice(512, 640))
FAR = -1e30
SCALE = 1.0 / math.sqrt(DIM)
LOG2_SCALE = SCALE * math.log2(math.e)
SHIFTS = (0, 1, -1, 2)
NN = (((1,), (0,)), ((), ()))
NT = (((1,), (1,)), ((), ()))


def dot(a, b, dims=NN):
    return lax.dot_general(a, b, dims, preferred_element_type=jnp.float32)


def flip(a):
    return jnp.transpose(a.astype(jnp.float32))


def rows_of(tile):
    return pl.ds(pl.multiple_of(tile * TILE, TILE), TILE)


def span_rows(ids, first, count, width):
    within = lax.broadcasted_iota(jnp.int32, (SPAN, width), 0)
    return jnp.concatenate([within + ids[first + s] * SPAN for s in range(count)], axis=0)


def seen(tile, key_ids, pair, ranges, query_feature, query_at):
    key_at = span_rows(key_ids, tile * TILE_SPANS, TILE_SPANS, PAIR)
    holds = (key_at >= ranges[0:1, :]) & (key_at < ranges[1:2, :])
    cover = dot(jnp.where(holds, 1.0, 0.0).astype(jnp.bfloat16), query_feature[pair])
    seen = cover > jnp.where(key_at <= query_at[pair, 0:1, :], 0.5, 63.5)
    return jnp.where(seen, 0.0, FAR)


def set_features(query_ids, ranges, query_feature, query_at):
    for pair in range(PAIRS):
        at = span_rows(query_ids, 2 * pair, 2, PAIR)
        holds = (at >= ranges[2:3, :]) & (at < ranges[3:4, :])
        weight = jnp.where(ranges[4:5, :] == 1, 64.0, 1.0)
        query_feature[pair] = flip(jnp.where(holds, weight, 0.0)).astype(jnp.bfloat16)
        query_at[pair] = jnp.transpose(at)[0:8, :]


def walk(order, counts, pair, step):
    whole, some = counts[2 * pair], counts[2 * pair + 1]

    def run(masked, size, first, steps):
        def body(i, _):
            at = pair * TILES + first + i * size
            step(masked, [order[at + t] for t in range(size)])
            return 0

        lax.fori_loop(0, steps, body, 0)
        return first + steps * size

    done = run(False, 4, 0, whole // 4)
    done = run(True, 4, done, (some - done) // 4)
    for size in (3, 2, 1):
        run(True, size, done, jnp.where(some - done == size, 1, 0))


def stack(ref, tiles):
    return jnp.concatenate([ref[rows_of(tile), :] for tile in tiles], axis=0)


def mask_of(tiles, *where):
    return jnp.concatenate([seen(tile, *where) for tile in tiles], axis=0)


def hide(mask, scores, heads):
    return scores + jnp.concatenate([mask] * heads, axis=1)


def pack_kernel(queries, out_grad, keys, values, qg, kv, row, sems):
    copies = [
        pltpu.make_async_copy(keys, row.at[:, :DIM], sems.at[0]),
        pltpu.make_async_copy(values, row.at[:, DIM:], sems.at[1]),
        pltpu.make_async_copy(queries, qg.at[:, :WIDTH], sems.at[2]),
        pltpu.make_async_copy(out_grad, qg.at[:, WIDTH:], sems.at[3]),
    ]
    for copy in copies:
        copy.start()
    for copy in copies[:2]:
        copy.wait()
    for i in range(PLANE):
        kv[i] = row[...]
    for copy in copies[2:]:
        copy.wait()


def join_kernel(a, b, c0, c1, c2, c3):
    for i, c in enumerate((c0, c1, c2, c3)):
        c[...] = (a[i].astype(jnp.float32) + b[i].astype(jnp.float32)).astype(jnp.bfloat16)


def finish_kernel(a0, a1, a2, a3, terms, out, query_grad, key_grad, value_grad):
    for at, to in ((0, out), (WIDTH, query_grad)):
        parts = [a[:, at:at + WIDTH].astype(jnp.float32) for a in (a0, a1, a2, a3)]
        to[...] = sum(parts).astype(jnp.bfloat16)
    for at, to in ((0, key_grad), (DIM, value_grad)):
        parts = [terms[i, :, at:at + DIM].astype(jnp.float32) for i in range(PLANE)]
        to[...] = sum(parts).astype(jnp.bfloat16)


def forward_kernel(
    order, counts, key_ids, key_rank, query_ids, query_rank,
    qg0, qg1, qg2, qg3, qg4, qg5, qg6, qg7, kv, ranges,
    total_out, top_out, stat_out, q_sorted, g_sorted, k_sorted, v_sorted,
    v_turned, stat, query_feature, query_at,
):
    set_features(query_ids, ranges, query_feature, query_at)
    for r, qg in enumerate((qg0, qg1, qg2, qg3, qg4, qg5, qg6, qg7)):
        for s in range(2):
            rank = query_rank[2 * r + s]
            pair, half = rank // 2, lax.rem(rank, 2)
            for h in range(HEADS):
                to = pl.ds(pl.multiple_of(h * PAIR + half * SPAN, SPAN), SPAN)
                q_at, g_at = h * DIM, (HEADS + h) * DIM
                q_sorted[pair, to, :] = qg[s * SPAN:(s + 1) * SPAN, q_at:q_at + DIM]
                g_sorted[pair, to, :] = qg[s * SPAN:(s + 1) * SPAN, g_at:g_at + DIM]

    def sort_keys(i, _):
        for s in range(2):
            rank = key_rank[2 * i + s]
            to = pl.ds(pl.multiple_of(rank * SPAN, SPAN), SPAN)
            rows = kv[i, s * SPAN:(s + 1) * SPAN, :]
            k_sorted[to, :] = rows[:, :DIM]
            v_sorted[to, :] = rows[:, DIM:]
        return 0

    lax.fori_loop(0, PLANE, sort_keys, 0)
    for t in range(TILES):
        v_turned[t] = jnp.transpose(v_sorted[t * TILE:(t + 1) * TILE, :])

    def one_pair(pair, _):
        total_out[pair] = jnp.zeros((DIM, LANES), jnp.float32)
        stat[0:1, :] = jnp.full((1, LANES), FAR, jnp.float32)
        stat[1:2, :] = jnp.zeros((1, LANES), jnp.float32)

        def step(masked, tiles):
            keys = stack(k_sorted, tiles)
            values = jnp.concatenate([v_turned[tile] for tile in tiles], axis=1)
            if masked:
                mask = mask_of(tiles, key_ids, pair, ranges, query_feature, query_at)
            raw = dot(keys, q_sorted[pair, GROUPS[0], :], NT)
            for i, group in enumerate(GROUPS):
                scores = raw * LOG2_SCALE
                if i + 1 < len(GROUPS):
                    raw = dot(keys, q_sorted[pair, GROUPS[i + 1], :], NT)
                if masked:
                    scores = hide(mask, scores, (group.stop - group.start) // PAIR)
                old = stat[0:1, group]
                new = jnp.maximum(old, jnp.max(scores, axis=0, keepdims=True))
                terms = jnp.exp2(scores - new)
                fade = jnp.exp2(old - new)
                stat[0:1, group] = new
                stat[1:2, group] = stat[1:2, group] * fade + jnp.sum(terms, axis=0, keepdims=True)
                total_out[pair, :, group] = total_out[pair, :, group] * fade + dot(
                    values, terms.astype(jnp.bfloat16)
                )

        walk(order, counts, pair, step)
        for h in range(HEADS):
            at = slice(h * PAIR, (h + 1) * PAIR)
            grad = jnp.transpose(g_sorted[pair, at, :]).astype(jnp.float32)
            stat[2:3, at] = jnp.sum(grad * total_out[pair, :, at], axis=0, keepdims=True)
        top, mass = stat[0:1, :], jnp.maximum(stat[1:2, :], 1e-30)
        top_out[pl.ds(pair, 1), :] = top
        stat_out[pl.ds(pair, 1), :] = top + jnp.log2(mass)
        stat_out[pl.ds(PAIRS + pair, 1), :] = stat[2:3, :] / mass
        return 0

    lax.fori_loop(0, PAIRS, one_pair, 0)


def merge(parts):
    logs, leans = [[part[k * PAIRS:(k + 1) * PAIRS, :] for part in parts] for k in range(2)]
    top = functools.reduce(jnp.maximum, logs)
    masses = [jnp.exp2(one - top) for one in logs]
    mass = sum(masses)
    lean = sum(one * part for one, part in zip(leans, masses))
    return top + jnp.log2(mass), lean / mass


def merge_kernel(s0, s1, s2, s3, out):
    for kind, rows in enumerate(merge([s0, s1, s2, s3])):
        out[kind * PAIRS:(kind + 1) * PAIRS, :] = rows


def turn_kernel(k_sorted, k_turned):
    for t in range(TILES):
        k_turned[t] = jnp.transpose(k_sorted[t * TILE:(t + 1) * TILE, :])


def give_back(query_rank, rows, outs, column):
    for r, out in enumerate(outs):
        for s in range(2):
            rank = query_rank[2 * r + s]
            at = pl.ds(pl.multiple_of(lax.rem(rank, 2) * SPAN, SPAN), SPAN)
            out[s * SPAN:(s + 1) * SPAN, column:column + WIDTH] = rows[rank // 2, at, :]


def backward_kernel(
    order, counts, key_ids, key_rank, query_ids, query_rank,
    q_sorted, g_sorted, k_sorted, v_sorted, k_turned, ranges, top_own, stat_mine, stat_other, total,
    od_mine, od_other, kv,
    key_total, value_total, query_total, rows, stat, query_feature, query_at,
):
    set_features(query_ids, ranges, query_feature, query_at)
    outs = [od.at[i] for od in (od_mine, od_other) for i in range(SIDE)]
    log_total, lean = merge([stat_mine, stat_other])
    share = jnp.exp2(top_own[...] - log_total)
    for pair in range(PAIRS):
        stat[pair, 0:1, :] = log_total[pair:pair + 1, :]
        stat[pair, 1:2, :] = lean[pair:pair + 1, :]
        for h in range(HEADS):
            at = slice(h * PAIR, (h + 1) * PAIR)
            scaled = total[pair, :, at] * share[pair:pair + 1, at]
            rows[pair, :, h * DIM:(h + 1) * DIM] = jnp.transpose(scaled.astype(jnp.bfloat16))
    give_back(query_rank, rows, outs, 0)

    query_total[...] = jnp.zeros_like(query_total)
    key_total[...] = jnp.zeros_like(key_total)
    value_total[...] = jnp.zeros_like(value_total)

    def one_pair(pair, _):
        def step(masked, tiles):
            keys, values = stack(k_sorted, tiles), stack(v_sorted, tiles)
            keys_turned = jnp.concatenate([k_turned[tile] for tile in tiles], axis=1)
            if masked:
                mask = mask_of(tiles, key_ids, pair, ranges, query_feature, query_at)

            def products(group):
                return (
                    dot(keys, q_sorted[pair, group, :], NT),
                    dot(values, g_sorted[pair, group, :], NT),
                )

            key_terms, value_terms = 0.0, 0.0
            raw, prob_grad = products(GROUPS[0])
            for i, group in enumerate(GROUPS):
                scores = raw * LOG2_SCALE - stat[pair, 0:1, group]
                lean = prob_grad - stat[pair, 1:2, group]
                if i + 1 < len(GROUPS):
                    raw, prob_grad = products(GROUPS[i + 1])
                if masked:
                    scores = hide(mask, scores, (group.stop - group.start) // PAIR)
                probs = jnp.exp2(scores)
                dscore = (probs * lean).astype(jnp.bfloat16)
                value_terms += dot(probs.astype(jnp.bfloat16), g_sorted[pair, group, :])
                key_terms += dot(dscore, q_sorted[pair, group, :])
                query_total[pair, :, group] += dot(keys_turned, dscore)
            for i, tile in enumerate(tiles):
                at = slice(i * TILE, (i + 1) * TILE)
                value_total[rows_of(tile), :] += value_terms[at]
                key_total[rows_of(tile), :] += key_terms[at]

        walk(order, counts, pair, step)
        return 0

    lax.fori_loop(0, PAIRS, one_pair, 0)

    def unsort_keys(i, _):
        for s in range(2):
            rank = key_rank[2 * i + s]
            at = pl.ds(pl.multiple_of(rank * SPAN, SPAN), SPAN)
            both = jnp.concatenate([key_total[at, :] * SCALE, value_total[at, :]], axis=1)
            kv[i, s * SPAN:(s + 1) * SPAN, :] = both.astype(jnp.bfloat16)
        return 0

    lax.fori_loop(0, PLANE, unsort_keys, 0)
    for pair in range(PAIRS):
        for h in range(HEADS):
            scaled = query_total[pair, :, h * PAIR:(h + 1) * PAIR] * SCALE
            rows[pair, :, h * DIM:(h + 1) * DIM] = jnp.transpose(scaled.astype(jnp.bfloat16))
    give_back(query_rank, rows, outs, WIDTH)


def shape(dims, dtype):
    return jax.ShapeDtypeStruct(dims, dtype)


def cost(matmuls):
    terms = PAIRS * LANES * KEYS // 2
    return pl.CostEstimate(
        flops=2 * matmuls * terms * DIM, bytes_accessed=8 * KEYS * DIM, transcendentals=terms
    )


SMEM = pl.BlockSpec(memory_space=pltpu.SMEM)
VMEM = pl.BlockSpec(memory_space=pltpu.VMEM)
HBM = pl.BlockSpec(memory_space=pltpu.HBM)


def ring(step):
    return [(i, i - i % SIDE + (i + step) % SIDE) for i in range(SIDE**3)]


def plan(mask_ranges, span_ids, place):
    line, z, core = place // SIDE, place % SIDE, lax.axis_index("grp")
    ids = span_ids.reshape(PLANE, SIDE, 2, 2)
    query_ids = jnp.concatenate(
        [ids[line, (z - step) % SIDE, side] for side in (core, 1 - core) for step in SHIFTS]
    )
    key_ids = ids[:, z, core].reshape(KEY_SPANS)

    def ranked(values):
        rank = jnp.sum((values[None, :] < values[:, None]).astype(jnp.int32), axis=1)
        at = jnp.arange(values.shape[0], dtype=jnp.int32)
        hit = (rank[:, None] == at[None, :]).astype(jnp.int32)
        return rank, jnp.sum(hit * values[:, None], axis=0)

    query_rank, query_sorted = ranked(query_ids)
    key_rank, key_sorted = ranked(key_ids)
    q_from, q_to, k_from, k_to, kind = [mask_ranges[:, column] for column in range(5)]
    q_low = jnp.maximum(query_sorted[:, None] * SPAN, q_from)
    q_high = jnp.minimum(query_sorted[:, None] * SPAN + SPAN, q_to)
    k_low = jnp.maximum(key_sorted[:, None] * SPAN, k_from)
    k_high = jnp.minimum(key_sorted[:, None] * SPAN + SPAN, k_to)
    some = (q_low < q_high)[:, None, :] & (k_low < k_high)[None, :, :]
    some = some & ((kind == 1) | (k_low[None, :, :] < q_high[:, None, :]))
    whole = (
        (q_high - q_low == SPAN)[:, None, :]
        & (k_high - k_low == SPAN)[None, :, :]
        & ((kind == 1) | (k_high[None, :, :] <= q_low[:, None, :] + 1))
    )
    by_tile = (PAIRS, 2, TILES, TILE_SPANS)
    some = jnp.any(some, axis=2).reshape(by_tile).any(axis=(1, 3))
    whole = jnp.any(whole, axis=2).reshape(by_tile).all(axis=(1, 3))
    tile_at = jnp.arange(TILES, dtype=jnp.int32)
    key = jnp.where(whole, 0, jnp.where(some, TILES, 2 * TILES)) + tile_at
    rank = jnp.sum((key[:, None, :] < key[:, :, None]).astype(jnp.int32), axis=2)
    order = jnp.sum(
        jnp.where(rank[:, :, None] == tile_at, tile_at[:, None], 0), axis=1
    ).reshape(PAIRS * TILES)
    counts = jnp.stack(
        [jnp.sum(which.astype(jnp.int32), axis=1) for which in (whole, some)], axis=1
    ).reshape(2 * PAIRS)
    columns = jnp.stack([k_from, k_to, q_from, q_to, kind])
    ranges = jnp.pad(columns, ((0, 3), (0, PAIR - kind.shape[0])))
    return order, counts, key_sorted, key_rank, query_sorted, query_rank, ranges


def kernel(body, name, scalars, operands, outs, scratch=(), matmuls=0, mebibytes=16, place=VMEM):
    return pl.pallas_call(
        body,
        out_shape=tuple(shape(*out) for out in outs),
        in_specs=[SMEM] * len(scalars) + [place] * len(operands),
        out_specs=(VMEM,) * len(outs),
        scratch_shapes=[pltpu.VMEM(*one) if isinstance(one, tuple) else one for one in scratch],
        compiler_params=pltpu.CompilerParams(vmem_limit_bytes=mebibytes * 1024 * 1024),
        cost_estimate=cost(matmuls) if matmuls else None,
        name=name,
    )(*scalars, *operands)


def per_device(queries, attn_keys, attn_values, out_grad, mask_ranges, span_ids):
    bf16, f32 = jnp.bfloat16, jnp.float32
    place = lax.axis_index("cp")
    planes = [[i * SIDE + z for i in range(PLANE)] for z in range(SIDE)]

    def swap(array):
        return lax.ppermute(array, "grp", [(0, 1), (1, 0)])

    def around(array, sign=1):
        return [lax.ppermute(array, "cp", ring(sign * step)) for step in SHIFTS[1:]]

    def plane_exchange(array):
        return lax.all_to_all(array, "cp", 0, 0, axis_index_groups=planes)

    sorted_shape = ((PAIRS, LANES, DIM), bf16)
    keys_shape = ((KEYS, DIM), bf16)
    kv_shape = ((PLANE, PAIR, 2 * DIM), bf16)
    line_shape = ((PAIR, 2 * WIDTH), bf16)
    lines_shape = ((SIDE, PAIR, 2 * WIDTH), bf16)
    tiles_shape = ((TILES, DIM, TILE), bf16)
    stat_shape = ((STAT_ROWS, LANES), f32)
    feature_shapes = [((PAIRS, PAIR, PAIR), bf16), ((PAIRS, 8, PAIR), jnp.int32)]

    qg, kv_copies = kernel(
        pack_kernel, "pack", [], [queries, out_grad, attn_keys, attn_values],
        [line_shape, kv_shape], [((PAIR, 2 * DIM), bf16), pltpu.SemaphoreType.DMA((4,))],
        mebibytes=60, place=HBM,
    )
    qg_parts = [qg] + around(qg)
    kv = plane_exchange(kv_copies)
    qg_parts += [swap(part) for part in qg_parts]
    order, counts, key_ids, key_rank, query_ids, query_rank, ranges = plan(
        mask_ranges, span_ids, place
    )
    lists = [order, counts, key_ids, key_rank, query_ids, query_rank]
    total, top, stat, q_sorted, g_sorted, k_sorted, v_sorted = kernel(
        forward_kernel, "forward", lists, [*qg_parts, kv, ranges],
        [((PAIRS, DIM, LANES), f32), ((PAIRS, LANES), f32), stat_shape, *[sorted_shape] * 2, *[keys_shape] * 2],
        [tiles_shape, ((8, LANES), f32), *feature_shapes],
        matmuls=2,
    )
    (k_turned,) = kernel(turn_kernel, "turn", [], [k_sorted], [tiles_shape])
    (stat_mine,) = kernel(merge_kernel, "merge", [], [stat, *around(stat)], [stat_shape])
    od_mine, od_other, kv_grad = kernel(
        backward_kernel, "backward", lists,
        [
            q_sorted, g_sorted, k_sorted, v_sorted, k_turned, ranges,
            top, stat_mine, swap(stat_mine), total,
        ],
        [lines_shape, lines_shape, kv_shape],
        [
            *[((KEYS, DIM), f32)] * 2, ((PAIRS, DIM, LANES), f32), ((PAIRS, PAIR, WIDTH), bf16),
            ((PAIRS, 8, LANES), f32), *feature_shapes,
        ],
        matmuls=5, mebibytes=28,
    )
    kv_terms = plane_exchange(kv_grad)
    od_other = swap(od_other)
    home = list(kernel(join_kernel, "join", [], [od_mine, od_other], [line_shape] * SIDE))
    home[1:] = [
        lax.ppermute(part, "cp", ring(-step)) for part, step in zip(home[1:], SHIFTS[1:])
    ]
    return kernel(
        finish_kernel, "finish", [], [*home, kv_terms],
        [((PAIR, WIDTH), bf16)] * 2 + [((PAIR, DIM), bf16)] * 2,
    )


def solution(mesh):
    rows = P(("cp", "grp"), None)
    return jax.shard_map(
        per_device,
        mesh=mesh,
        in_specs=(rows, rows, rows, rows, P(), P()),
        out_specs=(rows, rows, rows, rows),
        check_vma=False,
    )
```

```python
import functools
import math

import jax
import jax.numpy as jnp
from jax import lax
from jax.experimental import pallas as pl
from jax.experimental.pallas import tpu as pltpu
from jax.sharding import PartitionSpec as P

SIDE = 4
SPAN = 64
HEADS = 5
DIM = 128
PAIR = 2 * SPAN
LANES = HEADS * PAIR
PAIRS = 2 * SIDE
TILE = 128
TILE_SPANS = TILE // SPAN
PLANE = SIDE * SIDE
KEYS = PLANE * PAIR
KEY_SPANS = KEYS // SPAN
TILES = KEYS // TILE
STAT_ROWS = 2 * PAIRS
WIDTH = HEADS * DIM
GROUPS = (slice(0, 256), slice(256, 512), slice(512, 640))
FAR = -1e30
SAFE_LOG = 60.0
SCALE = 1.0 / math.sqrt(DIM)
LOG2_SCALE = SCALE * math.log2(math.e)
SHIFTS = (0, 1, -1, 2)
NN = (((1,), (0,)), ((), ()))
NT = (((1,), (1,)), ((), ()))


def dot(a, b, dims=NN):
    return lax.dot_general(a, b, dims, preferred_element_type=jnp.float32)


def flip(a):
    return jnp.transpose(a.astype(jnp.float32))


def rows_of(tile):
    return pl.ds(pl.multiple_of(tile * TILE, TILE), TILE)


def span_rows(ids, first, count, width):
    within = lax.broadcasted_iota(jnp.int32, (SPAN, width), 0)
    return jnp.concatenate([within + ids[first + s] * SPAN for s in range(count)], axis=0)


def seen(tile, key_ids, pair, ranges, query_feature, query_at):
    key_at = span_rows(key_ids, tile * TILE_SPANS, TILE_SPANS, PAIR)
    holds = (key_at >= ranges[0:1, :]) & (key_at < ranges[1:2, :])
    cover = dot(jnp.where(holds, 1.0, 0.0).astype(jnp.bfloat16), query_feature[pair])
    seen = cover > jnp.where(key_at <= query_at[pair, 0:1, :], 0.5, 63.5)
    return jnp.where(seen, 0.0, FAR)


def set_features(query_ids, ranges, query_feature, query_at):
    for pair in range(PAIRS):
        at = span_rows(query_ids, 2 * pair, 2, PAIR)
        holds = (at >= ranges[2:3, :]) & (at < ranges[3:4, :])
        weight = jnp.where(ranges[4:5, :] == 1, 64.0, 1.0)
        query_feature[pair] = flip(jnp.where(holds, weight, 0.0)).astype(jnp.bfloat16)
        query_at[pair] = jnp.transpose(at)[0:8, :]


def largest_norm(rows):
    sums = dot(rows * rows, jnp.ones((DIM, DIM), jnp.bfloat16))
    return jnp.max(sums.reshape(rows.shape[0] // 8, 8, DIM), axis=0)


def walk(order, counts, pair, step):
    whole, some = counts[2 * pair], counts[2 * pair + 1]

    def run(masked, size, first, steps):
        def body(i, _):
            at = pair * TILES + first + i * size
            step(masked, [order[at + t] for t in range(size)])
            return 0

        lax.fori_loop(0, steps, body, 0)
        return first + steps * size

    done = run(False, 4, 0, whole // 4)
    done = run(True, 4, done, (some - done) // 4)
    for size in (3, 2, 1):
        run(True, size, done, jnp.where(some - done == size, 1, 0))


def stack(ref, tiles):
    return jnp.concatenate([ref[rows_of(tile), :] for tile in tiles], axis=0)


def mask_of(tiles, *where):
    return jnp.concatenate([seen(tile, *where) for tile in tiles], axis=0)


def hide(mask, scores, heads):
    return scores + jnp.concatenate([mask] * heads, axis=1)


def pack_kernel(queries, out_grad, keys, values, qg, kv, row, sems):
    copies = [
        pltpu.make_async_copy(keys, row.at[:, :DIM], sems.at[0]),
        pltpu.make_async_copy(values, row.at[:, DIM:], sems.at[1]),
        pltpu.make_async_copy(queries, qg.at[:, :WIDTH], sems.at[2]),
        pltpu.make_async_copy(out_grad, qg.at[:, WIDTH:], sems.at[3]),
    ]
    for copy in copies:
        copy.start()
    for copy in copies[:2]:
        copy.wait()
    for i in range(PLANE):
        kv[i] = row[...]
    for copy in copies[2:]:
        copy.wait()


def join_kernel(a, b, c0, c1, c2, c3):
    for i, c in enumerate((c0, c1, c2, c3)):
        c[...] = (a[i].astype(jnp.float32) + b[i].astype(jnp.float32)).astype(jnp.bfloat16)


def finish_kernel(a0, a1, a2, a3, terms, out, query_grad, key_grad, value_grad):
    for at, to in ((0, out), (WIDTH, query_grad)):
        parts = [a[:, at:at + WIDTH].astype(jnp.float32) for a in (a0, a1, a2, a3)]
        to[...] = sum(parts).astype(jnp.bfloat16)
    for at, to in ((0, key_grad), (DIM, value_grad)):
        parts = [terms[i, :, at:at + DIM].astype(jnp.float32) for i in range(PLANE)]
        to[...] = sum(parts).astype(jnp.bfloat16)


def forward_kernel(
    order, counts, key_ids, key_rank, query_ids, query_rank,
    qg0, qg1, qg2, qg3, qg4, qg5, qg6, qg7, kv, ranges,
    total_out, top_out, stat_out, q_sorted, g_sorted, k_sorted, v_sorted,
    v_turned, stat, query_feature, query_at,
):
    set_features(query_ids, ranges, query_feature, query_at)
    for r, qg in enumerate((qg0, qg1, qg2, qg3, qg4, qg5, qg6, qg7)):
        for s in range(2):
            rank = query_rank[2 * r + s]
            pair, half = rank // 2, lax.rem(rank, 2)
            for h in range(HEADS):
                to = pl.ds(pl.multiple_of(h * PAIR + half * SPAN, SPAN), SPAN)
                q_at, g_at = h * DIM, (HEADS + h) * DIM
                q_sorted[pair, to, :] = qg[s * SPAN:(s + 1) * SPAN, q_at:q_at + DIM]
                g_sorted[pair, to, :] = qg[s * SPAN:(s + 1) * SPAN, g_at:g_at + DIM]

    def sort_keys(i, _):
        for s in range(2):
            rank = key_rank[2 * i + s]
            to = pl.ds(pl.multiple_of(rank * SPAN, SPAN), SPAN)
            rows = kv[i, s * SPAN:(s + 1) * SPAN, :]
            k_sorted[to, :] = rows[:, :DIM]
            v_sorted[to, :] = rows[:, DIM:]
        return 0

    lax.fori_loop(0, PLANE, sort_keys, 0)
    for t in range(TILES):
        v_turned[t] = jnp.transpose(v_sorted[t * TILE:(t + 1) * TILE, :])

    query_norm = functools.reduce(jnp.maximum, [largest_norm(q_sorted[p]) for p in range(PAIRS)])
    norms = [jnp.max(norm, axis=0, keepdims=True) for norm in (query_norm, largest_norm(k_sorted[...]))]
    small = jnp.max(norms[0] * norms[1]) * (1.02 * LOG2_SCALE**2) <= SAFE_LOG**2

    def one_pair(bounded, pair, _):
        total_out[pair] = jnp.zeros((DIM, LANES), jnp.float32)
        stat[0:1, :] = jnp.full((1, LANES), 0.0 if bounded else FAR, jnp.float32)
        stat[1:2, :] = jnp.zeros((1, LANES), jnp.float32)

        def step(masked, tiles):
            keys = stack(k_sorted, tiles)
            values = jnp.concatenate([v_turned[tile] for tile in tiles], axis=1)
            if masked:
                mask = mask_of(tiles, key_ids, pair, ranges, query_feature, query_at)
            raw = dot(keys, q_sorted[pair, GROUPS[0], :], NT)
            for i, group in enumerate(GROUPS):
                scores = raw * LOG2_SCALE
                if i + 1 < len(GROUPS):
                    raw = dot(keys, q_sorted[pair, GROUPS[i + 1], :], NT)
                if masked:
                    scores = hide(mask, scores, (group.stop - group.start) // PAIR)
                mass, total = stat[1:2, group], total_out[pair, :, group]
                if not bounded:
                    old = stat[0:1, group]
                    new = jnp.maximum(old, jnp.max(scores, axis=0, keepdims=True))
                    scores = scores - new
                    fade = jnp.exp2(old - new)
                    stat[0:1, group] = new
                    mass, total = mass * fade, total * fade
                terms = jnp.exp2(scores)
                stat[1:2, group] = mass + jnp.sum(terms, axis=0, keepdims=True)
                total_out[pair, :, group] = total + dot(values, terms.astype(jnp.bfloat16))

        walk(order, counts, pair, step)
        for h in range(HEADS):
            at = slice(h * PAIR, (h + 1) * PAIR)
            grad = jnp.transpose(g_sorted[pair, at, :]).astype(jnp.float32)
            stat[2:3, at] = jnp.sum(grad * total_out[pair, :, at], axis=0, keepdims=True)
        top, mass = stat[0:1, :], jnp.maximum(stat[1:2, :], 1e-30)
        top_out[pl.ds(pair, 1), :] = top
        stat_out[pl.ds(pair, 1), :] = top + jnp.log2(mass)
        stat_out[pl.ds(PAIRS + pair, 1), :] = stat[2:3, :] / mass
        return 0

    @pl.when(small)
    def _():
        lax.fori_loop(0, PAIRS, functools.partial(one_pair, True), 0)

    @pl.when(jnp.logical_not(small))
    def _():
        lax.fori_loop(0, PAIRS, functools.partial(one_pair, False), 0)


def merge(parts):
    logs, leans = [[part[k * PAIRS:(k + 1) * PAIRS, :] for part in parts] for k in range(2)]
    top = functools.reduce(jnp.maximum, logs)
    masses = [jnp.exp2(one - top) for one in logs]
    mass = sum(masses)
    lean = sum(one * part for one, part in zip(leans, masses))
    return top + jnp.log2(mass), lean / mass


def merge_kernel(s0, s1, s2, s3, out):
    for kind, rows in enumerate(merge([s0, s1, s2, s3])):
        out[kind * PAIRS:(kind + 1) * PAIRS, :] = rows


def turn_kernel(k_sorted, k_turned):
    for t in range(TILES):
        k_turned[t] = jnp.transpose(k_sorted[t * TILE:(t + 1) * TILE, :])


def give_back(query_rank, rows, outs, column):
    for r, out in enumerate(outs):
        for s in range(2):
            rank = query_rank[2 * r + s]
            at = pl.ds(pl.multiple_of(lax.rem(rank, 2) * SPAN, SPAN), SPAN)
            out[s * SPAN:(s + 1) * SPAN, column:column + WIDTH] = rows[rank // 2, at, :]


def backward_kernel(
    order, counts, key_ids, key_rank, query_ids, query_rank,
    q_sorted, g_sorted, k_sorted, v_sorted, k_turned, ranges, top_own, stat_mine, stat_other, total,
    od_mine, od_other, kv,
    key_total, value_total, query_total, rows, stat, query_feature, query_at,
):
    set_features(query_ids, ranges, query_feature, query_at)
    outs = [od.at[i] for od in (od_mine, od_other) for i in range(SIDE)]
    log_total, lean = merge([stat_mine, stat_other])
    share = jnp.exp2(top_own[...] - log_total)
    for pair in range(PAIRS):
        stat[pair, 0:1, :] = log_total[pair:pair + 1, :]
        stat[pair, 1:2, :] = lean[pair:pair + 1, :]
        for h in range(HEADS):
            at = slice(h * PAIR, (h + 1) * PAIR)
            scaled = total[pair, :, at] * share[pair:pair + 1, at]
            rows[pair, :, h * DIM:(h + 1) * DIM] = jnp.transpose(scaled.astype(jnp.bfloat16))
    give_back(query_rank, rows, outs, 0)

    query_total[...] = jnp.zeros_like(query_total)
    key_total[...] = jnp.zeros_like(key_total)
    value_total[...] = jnp.zeros_like(value_total)

    def one_pair(pair, _):
        def step(masked, tiles):
            keys, values = stack(k_sorted, tiles), stack(v_sorted, tiles)
            keys_turned = jnp.concatenate([k_turned[tile] for tile in tiles], axis=1)
            if masked:
                mask = mask_of(tiles, key_ids, pair, ranges, query_feature, query_at)

            def products(group):
                return (
                    dot(keys, q_sorted[pair, group, :], NT),
                    dot(values, g_sorted[pair, group, :], NT),
                )

            key_terms, value_terms = 0.0, 0.0
            raw, prob_grad = products(GROUPS[0])
            for i, group in enumerate(GROUPS):
                scores = raw * LOG2_SCALE - stat[pair, 0:1, group]
                lean = prob_grad - stat[pair, 1:2, group]
                if i + 1 < len(GROUPS):
                    raw, prob_grad = products(GROUPS[i + 1])
                if masked:
                    scores = hide(mask, scores, (group.stop - group.start) // PAIR)
                probs = jnp.exp2(scores)
                dscore = (probs * lean).astype(jnp.bfloat16)
                value_terms += dot(probs.astype(jnp.bfloat16), g_sorted[pair, group, :])
                key_terms += dot(dscore, q_sorted[pair, group, :])
                query_total[pair, :, group] += dot(keys_turned, dscore)
            for i, tile in enumerate(tiles):
                at = slice(i * TILE, (i + 1) * TILE)
                value_total[rows_of(tile), :] += value_terms[at]
                key_total[rows_of(tile), :] += key_terms[at]

        walk(order, counts, pair, step)
        return 0

    lax.fori_loop(0, PAIRS, one_pair, 0)

    def unsort_keys(i, _):
        for s in range(2):
            rank = key_rank[2 * i + s]
            at = pl.ds(pl.multiple_of(rank * SPAN, SPAN), SPAN)
            both = jnp.concatenate([key_total[at, :] * SCALE, value_total[at, :]], axis=1)
            kv[i, s * SPAN:(s + 1) * SPAN, :] = both.astype(jnp.bfloat16)
        return 0

    lax.fori_loop(0, PLANE, unsort_keys, 0)
    for pair in range(PAIRS):
        for h in range(HEADS):
            scaled = query_total[pair, :, h * PAIR:(h + 1) * PAIR] * SCALE
            rows[pair, :, h * DIM:(h + 1) * DIM] = jnp.transpose(scaled.astype(jnp.bfloat16))
    give_back(query_rank, rows, outs, WIDTH)


def shape(dims, dtype):
    return jax.ShapeDtypeStruct(dims, dtype)


def cost(matmuls):
    terms = PAIRS * LANES * KEYS // 2
    return pl.CostEstimate(
        flops=2 * matmuls * terms * DIM, bytes_accessed=8 * KEYS * DIM, transcendentals=terms
    )


SMEM = pl.BlockSpec(memory_space=pltpu.SMEM)
VMEM = pl.BlockSpec(memory_space=pltpu.VMEM)
HBM = pl.BlockSpec(memory_space=pltpu.HBM)


def ring(step):
    return [(i, i - i % SIDE + (i + step) % SIDE) for i in range(SIDE**3)]


def plan(mask_ranges, span_ids, place):
    line, z, core = place // SIDE, place % SIDE, lax.axis_index("grp")
    ids = span_ids.reshape(PLANE, SIDE, 2, 2)
    query_ids = jnp.concatenate(
        [ids[line, (z - step) % SIDE, side] for side in (core, 1 - core) for step in SHIFTS]
    )
    key_ids = ids[:, z, core].reshape(KEY_SPANS)

    def ranked(values):
        rank = jnp.sum((values[None, :] < values[:, None]).astype(jnp.int32), axis=1)
        at = jnp.arange(values.shape[0], dtype=jnp.int32)
        hit = (rank[:, None] == at[None, :]).astype(jnp.int32)
        return rank, jnp.sum(hit * values[:, None], axis=0)

    query_rank, query_sorted = ranked(query_ids)
    key_rank, key_sorted = ranked(key_ids)
    q_from, q_to, k_from, k_to, kind = [mask_ranges[:, column] for column in range(5)]
    q_low = jnp.maximum(query_sorted[:, None] * SPAN, q_from)
    q_high = jnp.minimum(query_sorted[:, None] * SPAN + SPAN, q_to)
    k_low = jnp.maximum(key_sorted[:, None] * SPAN, k_from)
    k_high = jnp.minimum(key_sorted[:, None] * SPAN + SPAN, k_to)
    some = (q_low < q_high)[:, None, :] & (k_low < k_high)[None, :, :]
    some = some & ((kind == 1) | (k_low[None, :, :] < q_high[:, None, :]))
    whole = (
        (q_high - q_low == SPAN)[:, None, :]
        & (k_high - k_low == SPAN)[None, :, :]
        & ((kind == 1) | (k_high[None, :, :] <= q_low[:, None, :] + 1))
    )
    by_tile = (PAIRS, 2, TILES, TILE_SPANS)
    some = jnp.any(some, axis=2).reshape(by_tile).any(axis=(1, 3))
    whole = jnp.any(whole, axis=2).reshape(by_tile).all(axis=(1, 3))
    tile_at = jnp.arange(TILES, dtype=jnp.int32)
    key = jnp.where(whole, 0, jnp.where(some, TILES, 2 * TILES)) + tile_at
    rank = jnp.sum((key[:, None, :] < key[:, :, None]).astype(jnp.int32), axis=2)
    order = jnp.sum(
        jnp.where(rank[:, :, None] == tile_at, tile_at[:, None], 0), axis=1
    ).reshape(PAIRS * TILES)
    counts = jnp.stack(
        [jnp.sum(which.astype(jnp.int32), axis=1) for which in (whole, some)], axis=1
    ).reshape(2 * PAIRS)
    columns = jnp.stack([k_from, k_to, q_from, q_to, kind])
    ranges = jnp.pad(columns, ((0, 3), (0, PAIR - kind.shape[0])))
    return order, counts, key_sorted, key_rank, query_sorted, query_rank, ranges


def kernel(body, name, scalars, operands, outs, scratch=(), matmuls=0, mebibytes=16, place=VMEM):
    return pl.pallas_call(
        body,
        out_shape=tuple(shape(*out) for out in outs),
        in_specs=[SMEM] * len(scalars) + [place] * len(operands),
        out_specs=(VMEM,) * len(outs),
        scratch_shapes=[pltpu.VMEM(*one) if isinstance(one, tuple) else one for one in scratch],
        compiler_params=pltpu.CompilerParams(vmem_limit_bytes=mebibytes * 1024 * 1024),
        cost_estimate=cost(matmuls) if matmuls else None,
        name=name,
    )(*scalars, *operands)


def per_device(queries, attn_keys, attn_values, out_grad, mask_ranges, span_ids):
    bf16, f32 = jnp.bfloat16, jnp.float32
    place = lax.axis_index("cp")
    planes = [[i * SIDE + z for i in range(PLANE)] for z in range(SIDE)]

    def swap(array):
        return lax.ppermute(array, "grp", [(0, 1), (1, 0)])

    def around(array, sign=1):
        return [lax.ppermute(array, "cp", ring(sign * step)) for step in SHIFTS[1:]]

    def plane_exchange(array):
        return lax.all_to_all(array, "cp", 0, 0, axis_index_groups=planes)

    sorted_shape = ((PAIRS, LANES, DIM), bf16)
    keys_shape = ((KEYS, DIM), bf16)
    kv_shape = ((PLANE, PAIR, 2 * DIM), bf16)
    line_shape = ((PAIR, 2 * WIDTH), bf16)
    lines_shape = ((SIDE, PAIR, 2 * WIDTH), bf16)
    tiles_shape = ((TILES, DIM, TILE), bf16)
    stat_shape = ((STAT_ROWS, LANES), f32)
    feature_shapes = [((PAIRS, PAIR, PAIR), bf16), ((PAIRS, 8, PAIR), jnp.int32)]

    qg, kv_copies = kernel(
        pack_kernel, "pack", [], [queries, out_grad, attn_keys, attn_values],
        [line_shape, kv_shape], [((PAIR, 2 * DIM), bf16), pltpu.SemaphoreType.DMA((4,))],
        mebibytes=60, place=HBM,
    )
    qg_parts = [qg] + around(qg)
    kv = plane_exchange(kv_copies)
    qg_parts += [swap(part) for part in qg_parts]
    order, counts, key_ids, key_rank, query_ids, query_rank, ranges = plan(
        mask_ranges, span_ids, place
    )
    lists = [order, counts, key_ids, key_rank, query_ids, query_rank]
    total, top, stat, q_sorted, g_sorted, k_sorted, v_sorted = kernel(
        forward_kernel, "forward", lists, [*qg_parts, kv, ranges],
        [((PAIRS, DIM, LANES), f32), ((PAIRS, LANES), f32), stat_shape, *[sorted_shape] * 2, *[keys_shape] * 2],
        [tiles_shape, ((8, LANES), f32), *feature_shapes],
        matmuls=2,
    )
    (k_turned,) = kernel(turn_kernel, "turn", [], [k_sorted], [tiles_shape])
    (stat_mine,) = kernel(merge_kernel, "merge", [], [stat, *around(stat)], [stat_shape])
    od_mine, od_other, kv_grad = kernel(
        backward_kernel, "backward", lists,
        [
            q_sorted, g_sorted, k_sorted, v_sorted, k_turned, ranges,
            top, stat_mine, swap(stat_mine), total,
        ],
        [lines_shape, lines_shape, kv_shape],
        [
            *[((KEYS, DIM), f32)] * 2, ((PAIRS, DIM, LANES), f32), ((PAIRS, PAIR, WIDTH), bf16),
            ((PAIRS, 8, LANES), f32), *feature_shapes,
        ],
        matmuls=5, mebibytes=28,
    )
    kv_terms = plane_exchange(kv_grad)
    od_other = swap(od_other)
    home = list(kernel(join_kernel, "join", [], [od_mine, od_other], [line_shape] * SIDE))
    home[1:] = [
        lax.ppermute(part, "cp", ring(-step)) for part, step in zip(home[1:], SHIFTS[1:])
    ]
    return kernel(
        finish_kernel, "finish", [], [*home, kv_terms],
        [((PAIR, WIDTH), bf16)] * 2 + [((PAIR, DIM), bf16)] * 2,
    )


def solution(mesh):
    rows = P(("cp", "grp"), None)
    return jax.shard_map(
        per_device,
        mesh=mesh,
        in_specs=(rows, rows, rows, rows, P(), P()),
        out_specs=(rows, rows, rows, rows),
        check_vma=False,
    )
```

```python
import functools
import math

import jax
import jax.numpy as jnp
from jax import lax
from jax.experimental import pallas as pl
from jax.experimental.pallas import tpu as pltpu
from jax.sharding import PartitionSpec as P

SIDE = 4
SPAN = 64
HEADS = 5
DIM = 128
PAIR = 2 * SPAN
LANES = HEADS * PAIR
PAIRS = 2 * SIDE
TILE = 128
TILE_SPANS = TILE // SPAN
PLANE = SIDE * SIDE
KEYS = PLANE * PAIR
KEY_SPANS = KEYS // SPAN
TILES = KEYS // TILE
STAT_ROWS = 2 * PAIRS
WIDTH = HEADS * DIM
GROUPS = (slice(0, 256), slice(256, 512), slice(512, 640))
FAR = -1e30
SAFE_LOG = 60.0
SCALE = 1.0 / math.sqrt(DIM)
LOG2_SCALE = SCALE * math.log2(math.e)
SHIFTS = (0, 1, -1, 2)
NN = (((1,), (0,)), ((), ()))
NT = (((1,), (1,)), ((), ()))


def dot(a, b, dims=NN):
    return lax.dot_general(a, b, dims, preferred_element_type=jnp.float32)


def flip(a):
    return jnp.transpose(a.astype(jnp.float32))


def rows_of(tile):
    return pl.ds(pl.multiple_of(tile * TILE, TILE), TILE)


def span_rows(ids, first, count, width):
    within = lax.broadcasted_iota(jnp.int32, (SPAN, width), 0)
    return jnp.concatenate([within + ids[first + s] * SPAN for s in range(count)], axis=0)


def seen(tile, key_ids, pair, ranges, query_feature, query_at):
    key_at = span_rows(key_ids, tile * TILE_SPANS, TILE_SPANS, PAIR)
    holds = (key_at >= ranges[0:1, :]) & (key_at < ranges[1:2, :])
    cover = dot(jnp.where(holds, 1.0, 0.0).astype(jnp.bfloat16), query_feature[pair])
    seen = cover > jnp.where(key_at <= query_at[pair, 0:1, :], 0.5, 63.5)
    return jnp.where(seen, 0.0, FAR)


def set_features(query_ids, ranges, query_feature, query_at):
    for pair in range(PAIRS):
        at = span_rows(query_ids, 2 * pair, 2, PAIR)
        holds = (at >= ranges[2:3, :]) & (at < ranges[3:4, :])
        weight = jnp.where(ranges[4:5, :] == 1, 64.0, 1.0)
        query_feature[pair] = flip(jnp.where(holds, weight, 0.0)).astype(jnp.bfloat16)
        query_at[pair] = jnp.transpose(at)[0:8, :]


def largest_norm(rows):
    sums = dot(rows * rows, jnp.ones((DIM, DIM), jnp.bfloat16))
    return jnp.max(sums.reshape(rows.shape[0] // 8, 8, DIM), axis=0)


def walk(order, counts, pair, step):
    whole, some = counts[2 * pair], counts[2 * pair + 1]

    def run(masked, size, first, steps):
        def body(i, _):
            at = pair * TILES + first + i * size
            step(masked, [order[at + t] for t in range(size)])
            return 0

        lax.fori_loop(0, steps, body, 0)
        return first + steps * size

    done = run(False, 4, 0, whole // 4)
    done = run(True, 4, done, (some - done) // 4)
    for size in (3, 2, 1):
        run(True, size, done, jnp.where(some - done == size, 1, 0))


def stack(ref, tiles):
    return jnp.concatenate([ref[rows_of(tile), :] for tile in tiles], axis=0)


def mask_of(tiles, *where):
    return jnp.concatenate([seen(tile, *where) for tile in tiles], axis=0)


def hide(mask, scores, heads):
    return scores + jnp.concatenate([mask] * heads, axis=1)


def pack_kernel(queries, out_grad, keys, values, qg, kv, row, sems):
    copies = [
        pltpu.make_async_copy(keys, row.at[:, :DIM], sems.at[0]),
        pltpu.make_async_copy(values, row.at[:, DIM:], sems.at[1]),
        pltpu.make_async_copy(queries, qg.at[:, :WIDTH], sems.at[2]),
        pltpu.make_async_copy(out_grad, qg.at[:, WIDTH:], sems.at[3]),
    ]
    for copy in copies:
        copy.start()
    for copy in copies[:2]:
        copy.wait()
    for i in range(PLANE):
        kv[i] = row[...]
    for copy in copies[2:]:
        copy.wait()


def join_kernel(a, b, c0, c1, c2, c3):
    for i, c in enumerate((c0, c1, c2, c3)):
        c[...] = (a[i].astype(jnp.float32) + b[i].astype(jnp.float32)).astype(jnp.bfloat16)


def finish_kernel(a0, a1, a2, a3, terms, out, query_grad, key_grad, value_grad):
    for at, to in ((0, out), (WIDTH, query_grad)):
        parts = [a[:, at:at + WIDTH].astype(jnp.float32) for a in (a0, a1, a2, a3)]
        to[...] = sum(parts).astype(jnp.bfloat16)
    for at, to in ((0, key_grad), (DIM, value_grad)):
        parts = [terms[i, :, at:at + DIM].astype(jnp.float32) for i in range(PLANE)]
        to[...] = sum(parts).astype(jnp.bfloat16)


def forward_kernel(
    order, counts, key_ids, key_rank, query_ids, query_rank,
    qg0, qg1, qg2, qg3, qg4, qg5, qg6, qg7, kv, ranges,
    total_out, top_out, stat_out, q_sorted, g_sorted, k_sorted, v_sorted,
    v_turned, stat, query_feature, query_at,
):
    set_features(query_ids, ranges, query_feature, query_at)
    for r, qg in enumerate((qg0, qg1, qg2, qg3, qg4, qg5, qg6, qg7)):
        for s in range(2):
            rank = query_rank[2 * r + s]
            pair, half = rank // 2, lax.rem(rank, 2)
            for h in range(HEADS):
                to = pl.ds(pl.multiple_of(h * PAIR + half * SPAN, SPAN), SPAN)
                q_at, g_at = h * DIM, (HEADS + h) * DIM
                q_sorted[pair, to, :] = qg[s * SPAN:(s + 1) * SPAN, q_at:q_at + DIM]
                g_sorted[pair, to, :] = qg[s * SPAN:(s + 1) * SPAN, g_at:g_at + DIM]

    def sort_keys(i, _):
        for s in range(2):
            rank = key_rank[2 * i + s]
            to = pl.ds(pl.multiple_of(rank * SPAN, SPAN), SPAN)
            rows = kv[i, s * SPAN:(s + 1) * SPAN, :]
            k_sorted[to, :] = rows[:, :DIM]
            v_sorted[to, :] = rows[:, DIM:]
        return 0

    lax.fori_loop(0, PLANE, sort_keys, 0)
    for t in range(TILES):
        v_turned[t] = jnp.transpose(v_sorted[t * TILE:(t + 1) * TILE, :])

    query_norm = functools.reduce(jnp.maximum, [largest_norm(q_sorted[p]) for p in range(PAIRS)])
    norms = [jnp.max(norm, axis=0, keepdims=True) for norm in (query_norm, largest_norm(k_sorted[...]))]
    small = jnp.max(norms[0] * norms[1]) * (1.02 * LOG2_SCALE**2) <= SAFE_LOG**2

    def one_pair(bounded, pair, _):
        total_out[pair] = jnp.zeros((DIM, LANES), jnp.float32)
        stat[0:1, :] = jnp.full((1, LANES), 0.0 if bounded else FAR, jnp.float32)
        stat[1:2, :] = jnp.zeros((1, LANES), jnp.float32)

        def step(masked, tiles):
            keys = stack(k_sorted, tiles)
            values = jnp.concatenate([v_turned[tile] for tile in tiles], axis=1)
            if masked:
                mask = mask_of(tiles, key_ids, pair, ranges, query_feature, query_at)
            raw = dot(keys, q_sorted[pair, GROUPS[0], :], NT)
            for i, group in enumerate(GROUPS):
                scores = raw * LOG2_SCALE
                if i + 1 < len(GROUPS):
                    raw = dot(keys, q_sorted[pair, GROUPS[i + 1], :], NT)
                if masked:
                    scores = hide(mask, scores, (group.stop - group.start) // PAIR)
                mass, total = stat[1:2, group], total_out[pair, :, group]
                if not bounded:
                    old = stat[0:1, group]
                    new = jnp.maximum(old, jnp.max(scores, axis=0, keepdims=True))
                    scores = scores - new
                    fade = jnp.exp2(old - new)
                    stat[0:1, group] = new
                    mass, total = mass * fade, total * fade
                terms = jnp.exp2(scores)
                stat[1:2, group] = mass + jnp.sum(terms, axis=0, keepdims=True)
                total_out[pair, :, group] = total + dot(values, terms.astype(jnp.bfloat16))

        walk(order, counts, pair, step)
        for h in range(HEADS):
            at = slice(h * PAIR, (h + 1) * PAIR)
            grad = jnp.transpose(g_sorted[pair, at, :]).astype(jnp.float32)
            stat[2:3, at] = jnp.sum(grad * total_out[pair, :, at], axis=0, keepdims=True)
        top, mass = stat[0:1, :], jnp.maximum(stat[1:2, :], 1e-30)
        top_out[pl.ds(pair, 1), :] = top
        stat_out[pl.ds(pair, 1), :] = top + jnp.log2(mass)
        stat_out[pl.ds(PAIRS + pair, 1), :] = stat[2:3, :] / mass
        return 0

    @pl.when(small)
    def _():
        lax.fori_loop(0, PAIRS, functools.partial(one_pair, True), 0)

    @pl.when(jnp.logical_not(small))
    def _():
        lax.fori_loop(0, PAIRS, functools.partial(one_pair, False), 0)


def merge(parts):
    logs, leans = [[part[k * PAIRS:(k + 1) * PAIRS, :] for part in parts] for k in range(2)]
    top = functools.reduce(jnp.maximum, logs)
    masses = [jnp.exp2(one - top) for one in logs]
    mass = sum(masses)
    lean = sum(one * part for one, part in zip(leans, masses))
    return top + jnp.log2(mass), lean / mass


def merge_kernel(s0, s1, s2, s3, out):
    for kind, rows in enumerate(merge([s0, s1, s2, s3])):
        out[kind * PAIRS:(kind + 1) * PAIRS, :] = rows


def turn_kernel(k_sorted, k_turned):
    for t in range(TILES):
        k_turned[t] = jnp.transpose(k_sorted[t * TILE:(t + 1) * TILE, :])


def give_back(query_rank, rows, outs, column):
    for r, out in enumerate(outs):
        for s in range(2):
            rank = query_rank[2 * r + s]
            at = pl.ds(pl.multiple_of(lax.rem(rank, 2) * SPAN, SPAN), SPAN)
            out[s * SPAN:(s + 1) * SPAN, column:column + WIDTH] = rows[rank // 2, at, :]


def backward_kernel(
    order, counts, key_ids, key_rank, query_ids, query_rank,
    q_sorted, g_sorted, k_sorted, v_sorted, k_turned, ranges, top_own, stat_mine, stat_other, total,
    od_mine, od_other, kv,
    key_total, value_total, query_total, rows, stat, query_feature, query_at,
):
    set_features(query_ids, ranges, query_feature, query_at)
    outs = [od.at[i] for od in (od_mine, od_other) for i in range(SIDE)]
    log_total, lean = merge([stat_mine, stat_other])
    share = jnp.exp2(top_own[...] - log_total)
    for pair in range(PAIRS):
        stat[pair, 0:1, :] = log_total[pair:pair + 1, :]
        stat[pair, 1:2, :] = lean[pair:pair + 1, :]
        for h in range(HEADS):
            at = slice(h * PAIR, (h + 1) * PAIR)
            scaled = total[pair, :, at] * share[pair:pair + 1, at]
            rows[pair, :, h * DIM:(h + 1) * DIM] = jnp.transpose(scaled.astype(jnp.bfloat16))
    give_back(query_rank, rows, outs, 0)

    query_total[...] = jnp.zeros_like(query_total)
    key_total[...] = jnp.zeros_like(key_total)
    value_total[...] = jnp.zeros_like(value_total)

    def one_pair(pair, _):
        def step(masked, tiles):
            keys, values = stack(k_sorted, tiles), stack(v_sorted, tiles)
            keys_turned = jnp.concatenate([k_turned[tile] for tile in tiles], axis=1)
            if masked:
                mask = mask_of(tiles, key_ids, pair, ranges, query_feature, query_at)

            def products(group):
                return (
                    dot(keys, q_sorted[pair, group, :], NT),
                    dot(values, g_sorted[pair, group, :], NT),
                )

            key_terms, value_terms = 0.0, 0.0
            raw, prob_grad = products(GROUPS[0])
            for i, group in enumerate(GROUPS):
                scores = raw * LOG2_SCALE - stat[pair, 0:1, group]
                lean = prob_grad - stat[pair, 1:2, group]
                if i + 1 < len(GROUPS):
                    raw, prob_grad = products(GROUPS[i + 1])
                if masked:
                    scores = hide(mask, scores, (group.stop - group.start) // PAIR)
                probs = jnp.exp2(scores)
                dscore = (probs * lean).astype(jnp.bfloat16)
                value_terms += dot(probs.astype(jnp.bfloat16), g_sorted[pair, group, :])
                key_terms += dot(dscore, q_sorted[pair, group, :])
                query_total[pair, :, group] += dot(keys_turned, dscore)
            for i, tile in enumerate(tiles):
                at = slice(i * TILE, (i + 1) * TILE)
                value_total[rows_of(tile), :] += value_terms[at]
                key_total[rows_of(tile), :] += key_terms[at]

        walk(order, counts, pair, step)
        return 0

    lax.fori_loop(0, PAIRS, one_pair, 0)

    def unsort_keys(i, _):
        for s in range(2):
            rank = key_rank[2 * i + s]
            at = pl.ds(pl.multiple_of(rank * SPAN, SPAN), SPAN)
            both = jnp.concatenate([key_total[at, :] * SCALE, value_total[at, :]], axis=1)
            kv[i, s * SPAN:(s + 1) * SPAN, :] = both.astype(jnp.bfloat16)
        return 0

    lax.fori_loop(0, PLANE, unsort_keys, 0)
    for pair in range(PAIRS):
        for h in range(HEADS):
            scaled = query_total[pair, :, h * PAIR:(h + 1) * PAIR] * SCALE
            rows[pair, :, h * DIM:(h + 1) * DIM] = jnp.transpose(scaled.astype(jnp.bfloat16))
    give_back(query_rank, rows, outs, WIDTH)


def shape(dims, dtype):
    return jax.ShapeDtypeStruct(dims, dtype)


def cost(matmuls):
    terms = PAIRS * LANES * KEYS // 2
    return pl.CostEstimate(
        flops=2 * matmuls * terms * DIM, bytes_accessed=8 * KEYS * DIM, transcendentals=terms
    )


SMEM = pl.BlockSpec(memory_space=pltpu.SMEM)
VMEM = pl.BlockSpec(memory_space=pltpu.VMEM)
HBM = pl.BlockSpec(memory_space=pltpu.HBM)


def ring(step):
    return [(i, i - i % SIDE + (i + step) % SIDE) for i in range(SIDE**3)]


def plan(mask_ranges, span_ids, place):
    line, z, core = place // SIDE, place % SIDE, lax.axis_index("grp")
    ids = span_ids.reshape(PLANE, SIDE, 2, 2)
    query_ids = jnp.concatenate(
        [ids[line, (z - step) % SIDE, side] for side in (core, 1 - core) for step in SHIFTS]
    )
    key_ids = ids[:, z, core].reshape(KEY_SPANS)

    def ranked(values):
        rank = jnp.sum((values[None, :] < values[:, None]).astype(jnp.int32), axis=1)
        at = jnp.arange(values.shape[0], dtype=jnp.int32)
        hit = (rank[:, None] == at[None, :]).astype(jnp.int32)
        return rank, jnp.sum(hit * values[:, None], axis=0)

    query_rank, query_sorted = ranked(query_ids)
    key_rank, key_sorted = ranked(key_ids)
    q_from, q_to, k_from, k_to, kind = [mask_ranges[:, column] for column in range(5)]
    q_low = jnp.maximum(query_sorted[:, None] * SPAN, q_from)
    q_high = jnp.minimum(query_sorted[:, None] * SPAN + SPAN, q_to)
    k_low = jnp.maximum(key_sorted[:, None] * SPAN, k_from)
    k_high = jnp.minimum(key_sorted[:, None] * SPAN + SPAN, k_to)
    some = (q_low < q_high)[:, None, :] & (k_low < k_high)[None, :, :]
    some = some & ((kind == 1) | (k_low[None, :, :] < q_high[:, None, :]))
    whole = (
        (q_high - q_low == SPAN)[:, None, :]
        & (k_high - k_low == SPAN)[None, :, :]
        & ((kind == 1) | (k_high[None, :, :] <= q_low[:, None, :] + 1))
    )
    by_tile = (PAIRS, 2, TILES, TILE_SPANS)
    some = jnp.any(some, axis=2).reshape(by_tile).any(axis=(1, 3))
    whole = jnp.any(whole, axis=2).reshape(by_tile).all(axis=(1, 3))
    tile_at = jnp.arange(TILES, dtype=jnp.int32)
    key = jnp.where(whole, 0, jnp.where(some, TILES, 2 * TILES)) + tile_at
    rank = jnp.sum((key[:, None, :] < key[:, :, None]).astype(jnp.int32), axis=2)
    order = jnp.sum(
        jnp.where(rank[:, :, None] == tile_at, tile_at[:, None], 0), axis=1
    ).reshape(PAIRS * TILES)
    counts = jnp.stack(
        [jnp.sum(which.astype(jnp.int32), axis=1) for which in (whole, some)], axis=1
    ).reshape(2 * PAIRS)
    columns = jnp.stack([k_from, k_to, q_from, q_to, kind])
    ranges = jnp.pad(columns, ((0, 3), (0, PAIR - kind.shape[0])))
    return order, counts, key_sorted, key_rank, query_sorted, query_rank, ranges


def kernel(body, name, scalars, operands, outs, scratch=(), matmuls=0, mebibytes=16, place=VMEM):
    return pl.pallas_call(
        body,
        out_shape=tuple(shape(*out) for out in outs),
        in_specs=[SMEM] * len(scalars) + [place] * len(operands),
        out_specs=(VMEM,) * len(outs),
        scratch_shapes=[pltpu.VMEM(*one) if isinstance(one, tuple) else one for one in scratch],
        compiler_params=pltpu.CompilerParams(vmem_limit_bytes=mebibytes * 1024 * 1024),
        cost_estimate=cost(matmuls) if matmuls else None,
        name=name,
    )(*scalars, *operands)


def per_device(queries, attn_keys, attn_values, out_grad, mask_ranges, span_ids):
    bf16, f32 = jnp.bfloat16, jnp.float32
    place = lax.axis_index("cp")
    planes = [[i * SIDE + z for i in range(PLANE)] for z in range(SIDE)]

    def swap(array):
        return lax.ppermute(array, "grp", [(0, 1), (1, 0)])

    def around(array, sign=1):
        return [lax.ppermute(array, "cp", ring(sign * step)) for step in SHIFTS[1:]]

    def plane_exchange(array):
        return lax.all_to_all(array, "cp", 0, 0, axis_index_groups=planes)

    sorted_shape = ((PAIRS, LANES, DIM), bf16)
    keys_shape = ((KEYS, DIM), bf16)
    kv_shape = ((PLANE, PAIR, 2 * DIM), bf16)
    line_shape = ((PAIR, 2 * WIDTH), bf16)
    lines_shape = ((SIDE, PAIR, 2 * WIDTH), bf16)
    tiles_shape = ((TILES, DIM, TILE), bf16)
    stat_shape = ((STAT_ROWS, LANES), f32)
    feature_shapes = [((PAIRS, PAIR, PAIR), bf16), ((PAIRS, 8, PAIR), jnp.int32)]

    qg, kv_copies = kernel(
        pack_kernel, "pack", [], [queries, out_grad, attn_keys, attn_values],
        [line_shape, kv_shape], [((PAIR, 2 * DIM), bf16), pltpu.SemaphoreType.DMA((4,))],
        mebibytes=60, place=HBM,
    )
    qg_parts = [qg] + around(qg)
    kv = plane_exchange(kv_copies)
    qg_late, qg_parts[1] = lax.optimization_barrier((qg, qg_parts[1]))
    qg_parts += [swap(part) for part in [qg_late] + qg_parts[1:]]
    order, counts, key_ids, key_rank, query_ids, query_rank, ranges = plan(
        mask_ranges, span_ids, place
    )
    lists = [order, counts, key_ids, key_rank, query_ids, query_rank]
    total, top, stat, q_sorted, g_sorted, k_sorted, v_sorted = kernel(
        forward_kernel, "forward", lists, [*qg_parts, kv, ranges],
        [((PAIRS, DIM, LANES), f32), ((PAIRS, LANES), f32), stat_shape, *[sorted_shape] * 2, *[keys_shape] * 2],
        [tiles_shape, ((8, LANES), f32), *feature_shapes],
        matmuls=2,
    )
    (k_turned,) = kernel(turn_kernel, "turn", [], [k_sorted], [tiles_shape])
    (stat_mine,) = kernel(merge_kernel, "merge", [], [stat, *around(stat)], [stat_shape])
    od_mine, od_other, kv_grad = kernel(
        backward_kernel, "backward", lists,
        [
            q_sorted, g_sorted, k_sorted, v_sorted, k_turned, ranges,
            top, stat_mine, swap(stat_mine), total,
        ],
        [lines_shape, lines_shape, kv_shape],
        [
            *[((KEYS, DIM), f32)] * 2, ((PAIRS, DIM, LANES), f32), ((PAIRS, PAIR, WIDTH), bf16),
            ((PAIRS, 8, LANES), f32), *feature_shapes,
        ],
        matmuls=5, mebibytes=28,
    )
    kv_terms = plane_exchange(kv_grad)
    od_other = swap(od_other)
    home = list(kernel(join_kernel, "join", [], [od_mine, od_other], [line_shape] * SIDE))
    home[1:] = [
        lax.ppermute(part, "cp", ring(-step)) for part, step in zip(home[1:], SHIFTS[1:])
    ]
    return kernel(
        finish_kernel, "finish", [], [*home, kv_terms],
        [((PAIR, WIDTH), bf16)] * 2 + [((PAIR, DIM), bf16)] * 2,
    )


def solution(mesh):
    rows = P(("cp", "grp"), None)
    return jax.shard_map(
        per_device,
        mesh=mesh,
        in_specs=(rows, rows, rows, rows, P(), P()),
        out_specs=(rows, rows, rows, rows),
        check_vma=False,
    )
```
